32 devices in a mesh: ctx: 8 (over y, x, core), head: 4 (over z).
Axes of the slice: x: 2, y: 2, z: 4, core: 2. Of those that a mesh axis runs over, the one named last changes fastest.
Arguments:
- queries: bfloat16 [4096, 2048], P(('ctx', 'head')), may hold values from -5.5 to 5.5
- key_vecs: bfloat16 [4096, 2048], P(('ctx', 'head')), may hold values from -5.5 to 5.5
- value_vecs: bfloat16 [4096, 2048], P(('ctx', 'head')), may hold values from -6 to 6
- out_grads: bfloat16 [4096, 2048], P(('ctx', 'head')), may hold values from -6 to 6
- local_offsets: int32 [32, 2], P('ctx'), may hold values from 0 to 3, as said below
- partner_pool: int32 [8, 2, 3], replicated, may hold values from 0 to 3, as said below
- partner_picks: int32 [32, 2, 2], P('ctx'), may hold values from 0 to 2, as said below
Outputs:
- query_grads: bfloat16 [4096, 2048], P(('ctx', 'head'))
- key_grads: bfloat16 [4096, 2048], P(('ctx', 'head'))
- value_grads: bfloat16 [4096, 2048], P(('ctx', 'head'))
The draws below stay inside these ranges and needn't reach their ends.
Inputs may be any that keep to these rules, and one draw needn't show every extreme that they name: `local_offsets`: each row holds 2 distinct offsets. `partner_pool`: each row of 3 entries names distinct blocks. `partner_picks`: each row of 2 entries holds distinct positions.
All inputs are finite; a program needn't handle non-finite values.
Results may differ from the reference program's by a relative error of at most 0.0069.
Values may be sent and summed in bfloat16 or wider, within the bound.
No kernel may reach another device: no remote copies, remote signals or barrier semaphores. Data moves between devices by JAX's collectives and lax.ppermute only.
A program may use at most 64 MiB of HBM per device.

```python
import jax
import jax.numpy as jnp
from jax import lax

H = 16
DH = 128
BLK = 128
BITS = 2
TOK_DEV = 128
TOKENS = 4096
NB = 4
NQB = 32
GROUPS = 8
LOCAL = 2
POOL = 3
GIVEN = 2
N_HEAD = 4


def distinct_rows(base_key, row_count, span_size, take_count):
    row_keys = jax.random.split(base_key, row_count)

    def shuffle_one(row_key):
        return jax.random.permutation(row_key, span_size).astype(jnp.int32)
    shuffled = jax.vmap(shuffle_one)(row_keys)
    top_pos = jnp.argmax(shuffled[0] == span_size - 1)
    shuffled = shuffled.at[0].set(jnp.roll(shuffled[0], -top_pos))
    if row_count > 1:
        low_pos = jnp.argmax(shuffled[1] == 0)
        shuffled = shuffled.at[1].set(jnp.roll(shuffled[1], -low_pos))
    return shuffled[:, :take_count]


def draw_queries(key, part):
    noise_key = jax.random.fold_in(key, 202)
    result = jnp.clip(1.5 * jax.random.normal(noise_key, (TOKENS, H * DH), jnp.float32), -5.5, 5.5)
    return result.astype(jnp.bfloat16)


def draw_key_vecs(key, part):
    noise_key = jax.random.fold_in(key, 303)
    result = jnp.clip(jax.random.normal(noise_key, (TOKENS, H * DH), jnp.float32), -5.5, 5.5)
    return result.astype(jnp.bfloat16)


def draw_local_offsets(key, part):
    folded = jax.random.fold_in(key, 404)
    return distinct_rows(folded, NQB, NB, LOCAL).astype(jnp.int32)


def draw_partner_pool(key, part):
    folded = jax.random.fold_in(key, 505)
    return distinct_rows(folded, GROUPS * BITS, NB, POOL).reshape(GROUPS, BITS, POOL)


def draw_partner_picks(key, part):
    folded = jax.random.fold_in(key, 606)
    return distinct_rows(folded, NQB * BITS, POOL, GIVEN).reshape(NQB, BITS, GIVEN)


def block_levels(own_key, shape, pieces, smallest, top_value):
    gain, own = 1.0, jax.random.fold_in(own_key, 6)
    for dim, parts in pieces:
        heights = jnp.exp(jax.random.uniform(jax.random.fold_in(own, dim), (parts,), jnp.float32, smallest / len(pieces), top_value / len(pieces)))
        gain = gain * jnp.repeat(heights, shape[dim] // parts).reshape([-1 if axis == dim else 1 for axis in range(len(shape))])
    return gain


def centred(own_key, extent, deviation, bound, pieces=(), kind=jnp.bfloat16):
    values = jax.random.normal(own_key, extent, jnp.float32) * deviation
    if len(pieces) > 0:
        values = block_levels(own_key, extent, pieces, -0.22, 0.18) * values
    return jnp.clip(values, min=-bound, max=bound).astype(kind)


def setup_inputs(seed: int = 0) -> dict:
    arg_keys = jax.random.split(jax.random.key(seed), 8)
    return {
        "queries": draw_queries(jax.random.fold_in(arg_keys[7], 71), 0),
        "key_vecs": draw_key_vecs(jax.random.fold_in(arg_keys[7], 71), 0),
        "value_vecs": centred(arg_keys[2], (TOKENS, H * DH), 1.0, 6.0, ((0, 32),)),
        "out_grads": centred(arg_keys[3], (TOKENS, H * DH), 1.0, 6.0, ((0, 32),)),
        "local_offsets": draw_local_offsets(jax.random.fold_in(arg_keys[7], 71), 0),
        "partner_pool": draw_partner_pool(jax.random.fold_in(arg_keys[7], 71), 0),
        "partner_picks": draw_partner_picks(jax.random.fold_in(arg_keys[7], 71), 0),
    }


def reference(queries, key_vecs, value_vecs, out_grads, local_offsets, partner_pool, partner_picks):
    blocks = TOK_DEV * N_HEAD // BLK
    block_total = TOKENS // BLK
    softmax_scale = DH ** -0.5
    query_f = queries.astype(jnp.float32).reshape(block_total, BLK, H, DH)
    key_f = key_vecs.astype(jnp.float32).reshape(block_total, BLK, H, DH)
    value_f = value_vecs.astype(jnp.float32).reshape(block_total, BLK, H, DH)
    grad_f = out_grads.astype(jnp.float32).reshape(block_total, BLK, H, DH)
    block_ids = jnp.arange(block_total, dtype=jnp.int32)
    groups = block_ids // blocks
    inner_idx = block_ids % blocks
    local_idx = groups[:, None] * blocks + (inner_idx[:, None] + local_offsets) % blocks
    bit_values = jnp.left_shift(jnp.int32(1), jnp.arange(BITS, dtype=jnp.int32))
    partners = jnp.bitwise_xor(groups[:, None], bit_values[None, :])
    pool_rows = partner_pool[groups]
    given_idx = jnp.take_along_axis(pool_rows, partner_picks, axis=2)
    remote_idx = partners[:, :, None] * blocks + given_idx
    key_index = jnp.concatenate([local_idx, remote_idx.reshape(block_total, -1)], axis=1).astype(jnp.int32)
    key_count = key_index.shape[1]

    def attend(carry_in, block_id):
        acc_key, acc_value = carry_in
        chosen = key_index[block_id]
        query_part = query_f[block_id]
        grad_part = grad_f[block_id]
        key_part = key_f[chosen].reshape(key_count * BLK, H, DH)
        value_part = value_f[chosen].reshape(key_count * BLK, H, DH)
        scores = jnp.einsum("qhd,khd->hqk", query_part, key_part) * softmax_scale
        row_max = jnp.max(scores, axis=-1, keepdims=True)
        exp_scores = jnp.exp(scores - row_max)
        weights = exp_scores / jnp.sum(exp_scores, axis=-1, keepdims=True)
        prob_grad = jnp.einsum("qhd,khd->hqk", grad_part, value_part)
        row_delta = jnp.sum(weights * prob_grad, axis=-1, keepdims=True)
        score_grad = lax.optimization_barrier((softmax_scale * weights * (prob_grad - row_delta)).astype(jnp.bfloat16)).astype(jnp.float32)
        weights_half = lax.optimization_barrier(weights.astype(jnp.bfloat16)).astype(jnp.float32)
        query_out = jnp.einsum("hqk,khd->qhd", score_grad, key_part)
        key_out = jnp.einsum("hqk,qhd->khd", score_grad, query_part)
        value_out = jnp.einsum("hqk,qhd->khd", weights_half, grad_part)
        acc_key = acc_key.at[chosen].add(key_out.reshape(key_count, BLK, H, DH))
        acc_value = acc_value.at[chosen].add(value_out.reshape(key_count, BLK, H, DH))
        return (acc_key, acc_value), query_out.astype(jnp.bfloat16)

    zeros_init = jnp.zeros((block_total, BLK, H, DH), jnp.float32)
    (acc_key, acc_value), query_rows = lax.scan(attend, (zeros_init, zeros_init), block_ids)
    query_grads = query_rows.reshape(TOKENS, H * DH)
    key_grads = acc_key.reshape(TOKENS, H * DH).astype(jnp.bfloat16)
    value_grads = acc_value.reshape(TOKENS, H * DH).astype(jnp.bfloat16)
    return query_grads, key_grads, value_grads
```

```python
import functools

import jax
import jax.numpy as jnp
from jax import lax
from jax.experimental import pallas as pl
from jax.experimental.pallas import tpu as pltpu
from jax.sharding import PartitionSpec as P

DH = 128
BLK = 128
LOG2_E = 1.4426950408889634
NT = (((1,), (1,)), ((), ()))


def swapped(value, axis, distance):
    return lax.ppermute(value, axis, [(i, i ^ 1 << distance) for i in range(lax.axis_size(axis))])


def rows(block):
    return pl.ds(pl.multiple_of(block * BLK, BLK), BLK)


def attend_kernel(
    index_ref, q_ref, k_ref, v_ref, g_ref, dq_ref, dk_ref, dv_ref, acc_k, acc_v, k_turned, k_cat, v_cat, kt_cat
):
    query_blocks = q_ref.shape[0] // BLK
    table_blocks = k_ref.shape[0] // BLK
    key_count = k_cat.shape[0] // BLK
    scale = DH**-0.5

    acc_k[...] = jnp.zeros_like(acc_k)
    acc_v[...] = jnp.zeros_like(acc_v)
    for block in range(table_blocks):
        k_turned[block] = k_ref[block * BLK : (block + 1) * BLK, :].T

    def step(block, _):
        query = q_ref[rows(block), :]
        grad = g_ref[rows(block), :]
        chosen = [index_ref[block * key_count + j] for j in range(key_count)]
        for j in range(key_count):
            part = slice(j * BLK, (j + 1) * BLK)
            k_cat[part, :] = k_ref[rows(chosen[j]), :]
            v_cat[part, :] = v_ref[rows(chosen[j]), :]
            kt_cat[:, part] = k_turned[chosen[j]]
        scores = lax.dot_general(k_cat[...], query, NT, preferred_element_type=jnp.float32)
        row_max = jnp.max(scores, axis=0, keepdims=True)
        exp_scores = jnp.exp2((scores - row_max) * (scale * LOG2_E))
        weights = exp_scores * (1.0 / jnp.sum(exp_scores, axis=0, keepdims=True))
        prob_grad = lax.dot_general(v_cat[...], grad, NT, preferred_element_type=jnp.float32)
        row_delta = jnp.sum(weights * prob_grad, axis=0, keepdims=True)
        score_grad = (scale * weights * (prob_grad - row_delta)).astype(jnp.bfloat16)
        weights_half = weights.astype(jnp.bfloat16)
        query_turned = jnp.dot(kt_cat[...], score_grad, preferred_element_type=jnp.float32)
        dq_ref[rows(block), :] = query_turned.T.astype(jnp.bfloat16)
        key_out = jnp.dot(score_grad, query, preferred_element_type=jnp.float32)
        value_out = jnp.dot(weights_half, grad, preferred_element_type=jnp.float32)
        for j in range(key_count):
            part = slice(j * BLK, (j + 1) * BLK)
            acc_k[rows(chosen[j]), :] += key_out[part]
            acc_v[rows(chosen[j]), :] += value_out[part]
        return 0

    lax.fori_loop(0, query_blocks, step, 0)
    dk_ref[...] = acc_k[...].astype(dk_ref.dtype)
    dv_ref[...] = acc_v[...].astype(dv_ref.dtype)


def attend(index, query, key, value, grad, table_type):
    heads = query.shape[1] // DH
    key_count = index.shape[1]
    tokens, table = query.shape[0], key.shape[0]
    token_spec = pl.BlockSpec((tokens, DH), lambda h, *_: (0, h))
    table_spec = pl.BlockSpec((table, DH), lambda h, *_: (0, h))
    return pl.pallas_call(
        attend_kernel,
        grid_spec=pltpu.PrefetchScalarGridSpec(
            num_scalar_prefetch=1,
            grid=(heads,),
            in_specs=[token_spec, table_spec, table_spec, token_spec],
            out_specs=[token_spec, table_spec, table_spec],
            scratch_shapes=[
                pltpu.VMEM((table, DH), jnp.float32),
                pltpu.VMEM((table, DH), jnp.float32),
                pltpu.VMEM((table // BLK, DH, BLK), jnp.bfloat16),
                pltpu.VMEM((key_count * BLK, DH), jnp.bfloat16),
                pltpu.VMEM((key_count * BLK, DH), jnp.bfloat16),
                pltpu.VMEM((DH, key_count * BLK), jnp.bfloat16),
            ],
        ),
        out_shape=[
            jax.ShapeDtypeStruct(query.shape, jnp.bfloat16),
            jax.ShapeDtypeStruct(key.shape, table_type),
            jax.ShapeDtypeStruct(key.shape, table_type),
        ],
        compiler_params=pltpu.CompilerParams(vmem_limit_bytes=40 << 20),
        name="attend",
    )(index.reshape(-1), query, key, value, grad)


def to_heads_kernel(*refs):
    *ins, out = refs
    for place, ref in enumerate(ins):
        for head in range(out.shape[0]):
            out[head, place] = ref[:, head * DH : (head + 1) * DH]


def from_heads_kernel(ref, *outs):
    for place, out in enumerate(outs):
        for head in range(ref.shape[0]):
            out[:, head * DH : (head + 1) * DH] = ref[head, place]


def whole_cluster(
    queries, key_vecs, value_vecs, out_grads, local_offsets, partner_pool, partner_picks
):
    bits = partner_pool.shape[1]
    groups, parts = lax.axis_size("ctx"), lax.axis_size("head")
    tokens, features = queries.shape
    cluster = (parts << bits)
    heads = features // DH // cluster
    members = [
        [group * parts + part for group in range(first, first + (1 << bits)) for part in range(parts)]
        for first in range(0, groups, 1 << bits)
    ]
    exchange = functools.partial(
        lax.all_to_all, axis_name=("ctx", "head"), split_axis=0, concat_axis=0, tiled=True, axis_index_groups=members
    )
    group = lax.axis_index("ctx")
    blocks = parts * (tokens // BLK)
    inner = jnp.arange(blocks, dtype=jnp.int32)
    place = jnp.bitwise_and(group, (1 << bits) - 1)
    own = place * blocks + (inner[:, None] + local_offsets) % blocks
    far = []
    for bit in range(bits):
        pool = partner_pool[group, bit]
        far.append(jnp.bitwise_xor(place, 1 << bit) * blocks + pool[partner_picks[:, bit]])
    index = jnp.concatenate([own] + far, axis=1).astype(jnp.int32)
    near = [list(range(first, first + (1 << bits))) for first in range(0, groups, 1 << bits)]
    index = lax.all_gather(index, "ctx", axis_index_groups=near, tiled=True)

    arrays = (queries, key_vecs, value_vecs, out_grads)
    packed = pl.pallas_call(
        to_heads_kernel,
        out_shape=jax.ShapeDtypeStruct((features // DH, len(arrays), tokens, DH), queries.dtype),
        name="to_heads",
    )(*arrays)
    packed = exchange(packed)
    query, key, value, grad = (packed[:, n].reshape(cluster * tokens, DH) for n in range(4))
    results = attend(index, query, key, value, grad, jnp.bfloat16)
    packed = jnp.stack([r.reshape(cluster, tokens, DH) for r in results], axis=1)
    packed = exchange(packed)
    return pl.pallas_call(
        from_heads_kernel,
        out_shape=[jax.ShapeDtypeStruct(queries.shape, queries.dtype)] * 3,
        name="from_heads",
    )(packed)


def by_pools(
    queries, key_vecs, value_vecs, out_grads, local_offsets, partner_pool, partner_picks
):
    to_heads = functools.partial(lax.all_to_all, axis_name="head", split_axis=1, concat_axis=0, tiled=True)
    to_tokens = functools.partial(lax.all_to_all, axis_name="head", split_axis=0, concat_axis=1, tiled=True)
    query, key, value, grad = (to_heads(x) for x in (queries, key_vecs, value_vecs, out_grads))
    width = query.shape[1]
    blocks = query.shape[0] // BLK
    bits, pool_size = partner_pool.shape[1:]
    group = lax.axis_index("ctx")
    asked = [partner_pool[jnp.bitwise_xor(group, 1 << bit), bit] for bit in range(bits)]

    def table(array):
        by_block = array.reshape(blocks, BLK, width)
        far = [swapped(by_block[asked[bit]], "ctx", bit) for bit in range(bits)]
        return jnp.concatenate([by_block] + far).reshape(-1, width)

    inner = jnp.arange(blocks, dtype=jnp.int32)
    own = (inner[:, None] + local_offsets) % blocks
    far = blocks + jnp.arange(bits, dtype=jnp.int32)[None, :, None] * pool_size + partner_picks
    index = jnp.concatenate([own, far.reshape(blocks, -1)], axis=1).astype(jnp.int32)
    dq, *tables = attend(index, query, table(key), table(value), grad, jnp.float32)
    grads = [dq]
    for array in tables:
        by_block = array.reshape(-1, BLK, width)
        total = by_block[:blocks]
        for bit in range(bits):
            lower = blocks + bit * pool_size
            back = swapped(by_block[lower : lower + pool_size], "ctx", bit)
            total = total.at[asked[bit]].add(back)
        grads.append(total.reshape(blocks * BLK, width).astype(jnp.bfloat16))
    return tuple(to_tokens(x) for x in grads)


def per_device(*args):
    partner_pool = args[5]
    cluster = lax.axis_size("head") << partner_pool.shape[1]
    if args[0].shape[1] // DH == cluster and args[0].shape[0] == BLK:
        return tuple(whole_cluster(*args))
    return by_pools(*args)


def solution(mesh):
    return jax.shard_map(
        per_device,
        mesh=mesh,
        in_specs=(
            P(("ctx", "head"), None),
            P(("ctx", "head"), None),
            P(("ctx", "head"), None),
            P(("ctx", "head"), None),
            P("ctx", None),
            P(),
            P("ctx", None, None),
        ),
        out_specs=(P(("ctx", "head"), None), P(("ctx", "head"), None), P(("ctx", "head"), None)),
        check_vma=False,
    )
```

```python
import functools

import jax
import jax.numpy as jnp
from jax import lax
from jax.experimental import pallas as pl
from jax.experimental.pallas import tpu as pltpu
from jax.sharding import PartitionSpec as P

DH = 128
BLK = 128
SCALE = DH**-0.5
LOG2_E = 1.4426950408889634
NT = (((1,), (1,)), ((), ()))
VMEM_BYTES = 16 << 20
IN_VMEM = pl.BlockSpec(memory_space=pltpu.VMEM)
IN_SMEM = pl.BlockSpec(memory_space=pltpu.SMEM)
INDEX_ROWS = 16


def swapped(value, axis, distance):
    return lax.ppermute(value, axis, [(i, i ^ distance) for i in range(lax.axis_size(axis))])


def rows(block):
    return pl.ds(block * BLK if isinstance(block, int) else pl.multiple_of(block * BLK, BLK), BLK)


def head_lanes(head):
    return pl.ds(pl.multiple_of(head * DH, DH), DH)


def local_call(kernel, out_shape, scalars, arrays, scratch=(), flops=0):
    moved = sum(x.size * x.dtype.itemsize for x in (*arrays, *jax.tree.leaves(out_shape)))
    return pl.pallas_call(
        kernel,
        out_shape=out_shape,
        in_specs=[IN_SMEM] * len(scalars) + [IN_VMEM] * len(arrays),
        out_specs=jax.tree.map(lambda _: IN_VMEM, out_shape),
        scratch_shapes=list(scratch),
        compiler_params=pltpu.CompilerParams(vmem_limit_bytes=VMEM_BYTES),
        cost_estimate=pl.CostEstimate(flops=flops, bytes_accessed=moved, transcendentals=0),
        name=getattr(kernel, "func", kernel).__name__,
    )(*scalars, *arrays)


def parts_of(blocks, count, extra=0):
    return [jax.ShapeDtypeStruct((blocks * BLK + extra, DH), jnp.bfloat16)] * count


def natural(me_ref, i, n, by, parts):
    k, j = (i, n) if by == "ctx" else (n, i)
    return jnp.bitwise_xor(me_ref[0], k) * parts + jnp.bitwise_xor(me_ref[1], j)


def pack(me_ref, *refs, arrays, others, by, parts):
    ins, outs = refs[:arrays], refs[arrays:]
    for i, out in enumerate(outs):
        for n in range(others):
            lanes = head_lanes(natural(me_ref, i, n, by, parts))
            for place, ref in enumerate(ins):
                out[rows(place * others + n), :] = ref[:, lanes]


def pack_with_index(me_ref, offsets_ref, pool_ref, picks_ref, *refs, parts, **kwargs):
    pack(me_ref, *refs, by="ctx", parts=parts, **kwargs)
    row = lax.broadcasted_iota(jnp.int32, (INDEX_ROWS, DH), 0)
    lane = lax.broadcasted_iota(jnp.int32, (INDEX_ROWS, DH), 1)
    tile = jnp.zeros((INDEX_ROWS, DH), jnp.int32)
    for block in range(parts):
        local = [offsets_ref[block, n] for n in range(offsets_ref.shape[1])]
        chosen = [me_ref[0] * parts + jnp.bitwise_and(block + offset, parts - 1) for offset in local]
        for bit in range(picks_ref.shape[1]):
            far = jnp.bitwise_xor(me_ref[0], 1 << bit) * parts
            for n in range(picks_ref.shape[2]):
                chosen.append(far + pool_ref[me_ref[2], bit, picks_ref[block, bit, n]])
        for n, value in enumerate(chosen):
            tile = jnp.where((row == block) & (lane == n), value, tile)
    for out in refs[kwargs["arrays"] :]:
        out[out.shape[0] - INDEX_ROWS :, :] = tile.astype(jnp.float32).astype(out.dtype)


def unpack(me_ref, *refs, by, parts):
    *ins, out = refs
    for i, ref in enumerate(ins):
        for n in range(ref.shape[0] // BLK):
            out[:, head_lanes(natural(me_ref, i, n, by, parts))] = ref[rows(n), :]


def pack_natural(*refs):
    *ins, out = refs
    for head in range(ins[0].shape[1] // DH):
        for place, ref in enumerate(ins):
            out[rows(head * len(ins) + place), :] = ref[:, head * DH : (head + 1) * DH]


def unpack_natural(ref, *outs):
    for head in range(outs[0].shape[1] // DH):
        for place, out in enumerate(outs):
            out[:, head * DH : (head + 1) * DH] = ref[rows(head * len(outs) + place), :]


def regroup(*refs, count, places):
    ins, outs = refs[:count], refs[count:]
    for i, out in enumerate(outs):
        for n, place in enumerate(places):
            for k, ref in enumerate(ins):
                out[rows(n * count + k), :] = ref[rows(place * len(outs) + i), :]


def regroup_with_index(*refs, count, places):
    *refs, index_ref = refs
    regroup(*refs, count=count, places=places)
    for k, ref in enumerate(refs[:count]):
        tile = ref[ref.shape[0] - INDEX_ROWS :, :]
        index_ref[k * INDEX_ROWS : (k + 1) * INDEX_ROWS, :] = tile.astype(jnp.float32).astype(jnp.int32)


def gather(me_ref, table, refs, by, parts, place=0):
    others = table.shape[0] // len(refs)
    for i, ref in enumerate(refs):
        for n in range(others):
            table[natural(me_ref, i, n, by, parts)] = ref[rows(place * others + n), :]


def spread(me_ref, table, refs, by, parts):
    others = table.shape[0] // len(refs)
    for i, ref in enumerate(refs):
        for n in range(others):
            ref[rows(n), :] = table[natural(me_ref, i, n, by, parts)].astype(ref.dtype)


def chosen_blocks(me_ref, index_ref, block, parts, key_count):
    group = jnp.bitwise_xor(lax.div(block, parts), me_ref[0])
    row = group * INDEX_ROWS + lax.rem(block, parts)
    return [index_ref[row, j] for j in range(key_count)]


def pair_of(block_of, first, second):
    return jnp.concatenate(
        [jnp.concatenate([block_of(a), block_of(b)], axis=1) for a, b in zip(first, second, strict=True)], axis=0
    )


def set_diagonal(ref, first, second):
    ref[:BLK, :DH] = first
    ref[BLK:, DH:] = second


def add_pair(acc, chosen, values):
    for half, blocks in enumerate(chosen):
        for j, block in enumerate(blocks):
            acc[block] += values[j * BLK : (j + 1) * BLK, half * DH : (half + 1) * DH]


def for_pairs(me_ref, index_ref, count, parts, key_count, unroll, one):
    def step(i, _):
        for slot in range(unroll):
            pair = i * unroll + slot
            blocks = (2 * pair, 2 * pair + 1)
            one(pair, slot, blocks, [chosen_blocks(me_ref, index_ref, b, parts, key_count) for b in blocks])
        return 0

    lax.fori_loop(0, count // unroll, step, 0)


def joined_block(ref, blocks, place):
    arrays = ref.shape[0] // (blocks * BLK)
    return lambda b: ref[rows(b * arrays + place), :]


def softmax_weights(me_ref, index_ref, joined_ref, w_ref, half_ref, q_diag, *, parts, near, key_count, unroll):
    query, key = (joined_block(joined_ref, near * parts, place) for place in range(2))
    q_diag[...] = jnp.zeros_like(q_diag)

    def one(pair, slot, blocks, chosen):
        set_diagonal(q_diag.at[slot], *map(query, blocks))
        keys = pair_of(key, *chosen)
        scores = lax.dot_general(keys, q_diag[slot], NT, preferred_element_type=jnp.float32)
        row_max = jnp.max(scores, axis=0, keepdims=True)
        exp_scores = jnp.exp2((scores - row_max) * (SCALE * LOG2_E))
        weights = exp_scores * (1.0 / jnp.sum(exp_scores, axis=0, keepdims=True))
        w_ref[pair] = weights
        half_ref[pair] = weights.astype(half_ref.dtype)

    for_pairs(me_ref, index_ref, w_ref.shape[0], parts, key_count, unroll, one)


def dv_parts(me_ref, index_ref, half_ref, *refs, parts, near, key_count, unroll):
    g_refs, dv_refs, (acc, g_table, g_diag) = refs[:parts], refs[parts : 2 * parts], refs[2 * parts :]
    gather(me_ref, g_table, g_refs, "head", parts)
    for ref in (acc, g_diag):
        ref[...] = jnp.zeros_like(ref)

    def one(pair, slot, blocks, chosen):
        set_diagonal(g_diag.at[slot], *(g_table[b] for b in blocks))
        add_pair(acc, chosen, jnp.dot(half_ref[pair], g_diag[slot], preferred_element_type=jnp.float32))

    for_pairs(me_ref, index_ref, half_ref.shape[0], parts, key_count, unroll, one)
    spread(me_ref, acc, dv_refs, "head", parts)


def dq_and_dk(me_ref, index_ref, joined_ref, *refs, parts, near, key_count, unroll):
    g_refs, v_refs, refs = refs[:parts], refs[parts : 2 * parts], refs[2 * parts :]
    w_ref, out_ref, acc, k_table, g_table, v_table, q_diag, g_diag = refs
    gather(me_ref, g_table, g_refs, "head", parts)
    gather(me_ref, v_table, v_refs, "head", parts)
    for ref in (acc, q_diag, g_diag):
        ref[...] = jnp.zeros_like(ref)
    query, key = (joined_block(joined_ref, near * parts, place) for place in range(2))
    for block in range(k_table.shape[0]):
        k_table[block] = key(block).T

    def one(pair, slot, blocks, chosen):
        set_diagonal(q_diag.at[slot], *map(query, blocks))
        set_diagonal(g_diag.at[slot], *(g_table[b] for b in blocks))
        values = pair_of(lambda b: v_table[b], *chosen)
        prob_grad = lax.dot_general(values, g_diag[slot], NT, preferred_element_type=jnp.float32)
        weights = w_ref[pair]
        row_delta = jnp.sum(weights * prob_grad, axis=0, keepdims=True)
        score_grad = (SCALE * (weights * (prob_grad - row_delta))).astype(jnp.bfloat16)
        add_pair(acc, chosen, jnp.dot(score_grad, q_diag[slot], preferred_element_type=jnp.float32))
        for half, block in enumerate(blocks):
            turned = jnp.concatenate([k_table[b] for b in chosen[half]], axis=1)
            own = score_grad[:, half * BLK : (half + 1) * BLK]
            grad = jnp.dot(turned, own, preferred_element_type=jnp.float32).T
            out_ref[rows(2 * block), :] = grad.astype(out_ref.dtype)

    for_pairs(me_ref, index_ref, w_ref.shape[0], parts, key_count, unroll, one)
    for block in range(acc.shape[0]):
        out_ref[rows(2 * block + 1), :] = acc[block].astype(out_ref.dtype)


def whole_cluster(
    queries, key_vecs, value_vecs, out_grads, local_offsets, partner_pool, partner_picks
):
    bits = partner_pool.shape[1]
    parts = lax.axis_size("head")
    near = 1 << bits
    cluster = near * parts
    key_count = local_offsets.shape[1] + bits * partner_picks.shape[2]
    group = lax.axis_index("ctx")
    me = jnp.stack([jnp.bitwise_and(group, near - 1), lax.axis_index("head"), group]).astype(jnp.int32)

    def over_ctx(by_part):
        return [x if k == 0 else swapped(x, "ctx", k) for k, x in enumerate(by_part)]

    def over_head(by_part):
        return [x if j == 0 else swapped(x, "head", j) for j, x in enumerate(by_part)]

    members = [
        [member * parts + part for member in range(first, first + near) for part in range(parts)]
        for first in range(0, lax.axis_size("ctx"), near)
    ]
    exchange = functools.partial(
        lax.all_to_all, axis_name=("ctx", "head"), split_axis=0, concat_axis=0, tiled=True, axis_index_groups=members
    )
    joined = local_call(pack_natural, parts_of(2 * cluster, 1)[0], (), (queries, key_vecs))
    later = (out_grads, value_vecs, local_offsets, partner_pool, partner_picks)
    joined, later = lax.optimization_barrier((joined, later))
    out_grads, value_vecs, local_offsets, partner_pool, partner_picks = later
    joined = exchange(joined)
    grad = local_call(
        functools.partial(pack, arrays=1, others=parts, by="ctx", parts=parts), parts_of(parts, near), (me,), (out_grads,)
    )
    grad = local_call(functools.partial(regroup, count=near, places=[0]), parts_of(near, parts), (), over_ctx(grad))
    grad = over_head(grad)
    value = local_call(
        functools.partial(pack_with_index, arrays=1, others=parts, parts=parts),
        parts_of(parts, near, INDEX_ROWS),
        (me, local_offsets, partner_pool, partner_picks),
        (value_vecs,),
    )
    *value, index = local_call(
        functools.partial(regroup_with_index, count=near, places=[0]),
        parts_of(near, parts) + [jax.ShapeDtypeStruct((near * INDEX_ROWS, DH), jnp.int32)],
        (),
        over_ctx(value),
    )
    joined, value = lax.optimization_barrier((joined, value))
    value = over_head(value)

    pairs, keys = cluster // 2, key_count * BLK
    unroll = 4 if pairs % 4 == 0 else 1
    kwargs = dict(parts=parts, near=near, key_count=key_count, unroll=unroll)
    flops = 4 * cluster * keys * BLK * DH
    acc, table = (pltpu.VMEM((cluster, BLK, DH), dtype) for dtype in (jnp.float32, jnp.bfloat16))
    diagonal = pltpu.VMEM((unroll, 2 * BLK, 2 * DH), jnp.bfloat16)
    weights, half = local_call(
        functools.partial(softmax_weights, **kwargs),
        [jax.ShapeDtypeStruct((pairs, keys, 2 * BLK), dtype) for dtype in (jnp.float32, jnp.bfloat16)],
        (me, index),
        (joined,),
        [diagonal],
        flops // 2,
    )
    dv = local_call(
        functools.partial(dv_parts, **kwargs),
        parts_of(near, parts),
        (me, index),
        (half, *grad),
        [acc, table, diagonal],
        flops // 2,
    )
    dv = over_head(dv)
    joined = local_call(
        functools.partial(dq_and_dk, **kwargs),
        parts_of(2 * cluster, 1)[0],
        (me, index),
        (joined, *grad, *value, weights),
        [acc] + [table] * 3 + [diagonal] * 2,
        flops * 3 // 2,
    )
    joined, dv = lax.optimization_barrier((joined, dv))
    joined = exchange(joined)
    dv = local_call(functools.partial(regroup, count=parts, places=[0]), parts_of(parts, near), (), dv)
    dv = over_ctx(dv)
    out = jax.ShapeDtypeStruct(queries.shape, queries.dtype)
    value_grads = local_call(functools.partial(unpack, by="ctx", parts=parts), out, (me,), dv)
    query_grads, key_grads = local_call(unpack_natural, [out] * 2, (), (joined,))
    return query_grads, key_grads, value_grads


def attend_kernel(
    index_ref, q_ref, k_ref, v_ref, g_ref, dq_ref, dk_ref, dv_ref, acc_k, acc_v, k_turned, k_cat, v_cat, kt_cat
):
    query_blocks = q_ref.shape[0] // BLK
    table_blocks = k_ref.shape[0] // BLK
    key_count = k_cat.shape[0] // BLK

    acc_k[...] = jnp.zeros_like(acc_k)
    acc_v[...] = jnp.zeros_like(acc_v)
    for block in range(table_blocks):
        k_turned[block] = k_ref[block * BLK : (block + 1) * BLK, :].T

    def step(block, _):
        query = q_ref[rows(block), :]
        grad = g_ref[rows(block), :]
        chosen = [index_ref[block * key_count + j] for j in range(key_count)]
        for j in range(key_count):
            part = slice(j * BLK, (j + 1) * BLK)
            k_cat[part, :] = k_ref[rows(chosen[j]), :]
            v_cat[part, :] = v_ref[rows(chosen[j]), :]
            kt_cat[:, part] = k_turned[chosen[j]]
        scores = lax.dot_general(k_cat[...], query, NT, preferred_element_type=jnp.float32)
        row_max = jnp.max(scores, axis=0, keepdims=True)
        exp_scores = jnp.exp2((scores - row_max) * (SCALE * LOG2_E))
        weights = exp_scores * (1.0 / jnp.sum(exp_scores, axis=0, keepdims=True))
        prob_grad = lax.dot_general(v_cat[...], grad, NT, preferred_element_type=jnp.float32)
        row_delta = jnp.sum(weights * prob_grad, axis=0, keepdims=True)
        score_grad = (SCALE * weights * (prob_grad - row_delta)).astype(jnp.bfloat16)
        weights_half = weights.astype(jnp.bfloat16)
        query_turned = jnp.dot(kt_cat[...], score_grad, preferred_element_type=jnp.float32)
        dq_ref[rows(block), :] = query_turned.T.astype(jnp.bfloat16)
        key_out = jnp.dot(score_grad, query, preferred_element_type=jnp.float32)
        value_out = jnp.dot(weights_half, grad, preferred_element_type=jnp.float32)
        for j in range(key_count):
            part = slice(j * BLK, (j + 1) * BLK)
            acc_k[rows(chosen[j]), :] += key_out[part]
            acc_v[rows(chosen[j]), :] += value_out[part]
        return 0

    lax.fori_loop(0, query_blocks, step, 0)
    dk_ref[...] = acc_k[...].astype(dk_ref.dtype)
    dv_ref[...] = acc_v[...].astype(dv_ref.dtype)


def attend(index, query, key, value, grad, table_type):
    heads = query.shape[1] // DH
    key_count = index.shape[1]
    tokens, table = query.shape[0], key.shape[0]
    token_spec = pl.BlockSpec((tokens, DH), lambda h, *_: (0, h))
    table_spec = pl.BlockSpec((table, DH), lambda h, *_: (0, h))
    return pl.pallas_call(
        attend_kernel,
        grid_spec=pltpu.PrefetchScalarGridSpec(
            num_scalar_prefetch=1,
            grid=(heads,),
            in_specs=[token_spec, table_spec, table_spec, token_spec],
            out_specs=[token_spec, table_spec, table_spec],
            scratch_shapes=[
                pltpu.VMEM((table, DH), jnp.float32),
                pltpu.VMEM((table, DH), jnp.float32),
                pltpu.VMEM((table // BLK, DH, BLK), jnp.bfloat16),
                pltpu.VMEM((key_count * BLK, DH), jnp.bfloat16),
                pltpu.VMEM((key_count * BLK, DH), jnp.bfloat16),
                pltpu.VMEM((DH, key_count * BLK), jnp.bfloat16),
            ],
        ),
        out_shape=[
            jax.ShapeDtypeStruct(query.shape, jnp.bfloat16),
            jax.ShapeDtypeStruct(key.shape, table_type),
            jax.ShapeDtypeStruct(key.shape, table_type),
        ],
        compiler_params=pltpu.CompilerParams(vmem_limit_bytes=VMEM_BYTES),
        name="attend",
    )(index.reshape(-1), query, key, value, grad)


def by_pools(
    queries, key_vecs, value_vecs, out_grads, local_offsets, partner_pool, partner_picks
):
    to_heads = functools.partial(lax.all_to_all, axis_name="head", split_axis=1, concat_axis=0, tiled=True)
    to_tokens = functools.partial(lax.all_to_all, axis_name="head", split_axis=0, concat_axis=1, tiled=True)
    query, key, value, grad = (to_heads(x) for x in (queries, key_vecs, value_vecs, out_grads))
    width = query.shape[1]
    blocks = query.shape[0] // BLK
    bits, pool_size = partner_pool.shape[1:]
    group = lax.axis_index("ctx")
    asked = [partner_pool[jnp.bitwise_xor(group, 1 << bit), bit] for bit in range(bits)]

    def table(array):
        by_block = array.reshape(blocks, BLK, width)
        far = [swapped(by_block[asked[bit]], "ctx", 1 << bit) for bit in range(bits)]
        return jnp.concatenate([by_block] + far).reshape(-1, width)

    inner = jnp.arange(blocks, dtype=jnp.int32)
    own = (inner[:, None] + local_offsets) % blocks
    far = blocks + jnp.arange(bits, dtype=jnp.int32)[None, :, None] * pool_size + partner_picks
    index = jnp.concatenate([own, far.reshape(blocks, -1)], axis=1).astype(jnp.int32)
    dq, *tables = attend(index, query, table(key), table(value), grad, jnp.float32)
    grads = [dq]
    for array in tables:
        by_block = array.reshape(-1, BLK, width)
        total = by_block[:blocks]
        for bit in range(bits):
            lower = blocks + bit * pool_size
            back = swapped(by_block[lower : lower + pool_size], "ctx", 1 << bit)
            total = total.at[asked[bit]].add(back)
        grads.append(total.reshape(blocks * BLK, width).astype(jnp.bfloat16))
    return tuple(to_tokens(x) for x in grads)


def per_device(*args):
    tokens, features = args[0].shape
    parts = lax.axis_size("head")
    cluster = parts << args[5].shape[1]
    if features // DH == cluster and tokens == BLK and parts & (parts - 1) == 0 and 1 < parts <= INDEX_ROWS:
        return whole_cluster(*args)
    return by_pools(*args)


def solution(mesh):
    return jax.shard_map(
        per_device,
        mesh=mesh,
        in_specs=(
            P(("ctx", "head"), None),
            P(("ctx", "head"), None),
            P(("ctx", "head"), None),
            P(("ctx", "head"), None),
            P("ctx", None),
            P(),
            P("ctx", None, None),
        ),
        out_specs=(P(("ctx", "head"), None), P(("ctx", "head"), None), P(("ctx", "head"), None)),
        check_vma=False,
    )
```

```python
import functools

import jax
import jax.numpy as jnp
from jax import lax
from jax.experimental import pallas as pl
from jax.experimental.pallas import tpu as pltpu
from jax.sharding import PartitionSpec as P

DH = 128
BLK = 128
SCALE = DH**-0.5
LOG2_E = 1.4426950408889634
NT = (((1,), (1,)), ((), ()))
TN = (((0,), (0,)), ((), ()))
VMEM_BYTES = 16 << 20
IN_VMEM = pl.BlockSpec(memory_space=pltpu.VMEM)
IN_SMEM = pl.BlockSpec(memory_space=pltpu.SMEM)
INDEX_ROWS = 16


def swapped(value, axis, distance):
    return lax.ppermute(value, axis, [(i, i ^ distance) for i in range(lax.axis_size(axis))])


def rows(block):
    return pl.ds(block * BLK if isinstance(block, int) else pl.multiple_of(block * BLK, BLK), BLK)


def head_lanes(head):
    return pl.ds(pl.multiple_of(head * DH, DH), DH)


def local_call(kernel, out_shape, scalars, arrays, scratch=(), flops=0):
    moved = sum(x.size * x.dtype.itemsize for x in (*arrays, *jax.tree.leaves(out_shape)))
    return pl.pallas_call(
        kernel,
        out_shape=out_shape,
        in_specs=[IN_SMEM] * len(scalars) + [IN_VMEM] * len(arrays),
        out_specs=jax.tree.map(lambda _: IN_VMEM, out_shape),
        scratch_shapes=list(scratch),
        compiler_params=pltpu.CompilerParams(vmem_limit_bytes=VMEM_BYTES),
        cost_estimate=pl.CostEstimate(flops=flops, bytes_accessed=moved, transcendentals=0),
        name=getattr(kernel, "func", kernel).__name__,
    )(*scalars, *arrays)


def parts_of(blocks, count, extra=0):
    return [jax.ShapeDtypeStruct((blocks * BLK + extra, DH), jnp.bfloat16)] * count


def natural(me_ref, i, n, by, near):
    k, j = (i, n) if by == "ctx" else (n, i)
    return jnp.bitwise_xor(me_ref[1], j) * near + jnp.bitwise_xor(me_ref[0], k)


def pack(me_ref, *refs, arrays, others, by, near):
    ins, outs = refs[:arrays], refs[arrays:]
    for i, out in enumerate(outs):
        for n in range(others):
            lanes = head_lanes(natural(me_ref, i, n, by, near))
            for place, ref in enumerate(ins):
                out[rows(place * others + n), :] = ref[:, lanes]


def pack_with_index(me_ref, offsets_ref, pool_ref, picks_ref, *refs, parts, near, **kwargs):
    pack(me_ref, *refs, by="ctx", near=near, **kwargs)
    row = lax.broadcasted_iota(jnp.int32, (INDEX_ROWS, DH), 0)
    lane = lax.broadcasted_iota(jnp.int32, (INDEX_ROWS, DH), 1)
    tile = jnp.zeros((INDEX_ROWS, DH), jnp.int32)
    for block in range(parts):
        local = [offsets_ref[block, n] for n in range(offsets_ref.shape[1])]
        chosen = [jnp.bitwise_and(block + offset, parts - 1) * near + me_ref[0] for offset in local]
        for bit in range(picks_ref.shape[1]):
            far = jnp.bitwise_xor(me_ref[0], 1 << bit)
            for n in range(picks_ref.shape[2]):
                chosen.append(pool_ref[me_ref[2], bit, picks_ref[block, bit, n]] * near + far)
        for n, value in enumerate(chosen):
            tile = jnp.where((row == block) & (lane == n), value, tile)
    for out in refs[kwargs["arrays"] :]:
        out[out.shape[0] - INDEX_ROWS :, :] = tile.astype(jnp.float32).astype(out.dtype)


def unpack(me_ref, *refs, by, near):
    *ins, out = refs
    for i, ref in enumerate(ins):
        for n in range(ref.shape[0] // BLK):
            out[:, head_lanes(natural(me_ref, i, n, by, near))] = ref[rows(n), :]


def pack_natural(*refs):
    *ins, out = refs
    for head in range(ins[0].shape[1] // DH):
        for place, ref in enumerate(ins):
            out[rows(head * len(ins) + place), :] = ref[:, head * DH : (head + 1) * DH]


def unpack_natural(ref, *outs):
    for head in range(outs[0].shape[1] // DH):
        for place, out in enumerate(outs):
            out[:, head * DH : (head + 1) * DH] = ref[rows(head * len(outs) + place), :]


def regroup(*refs, count, places):
    ins, outs = refs[:count], refs[count:]
    for i, out in enumerate(outs):
        for n, place in enumerate(places):
            for k, ref in enumerate(ins):
                out[rows(n * count + k), :] = ref[rows(place * len(outs) + i), :]


def regroup_with_index(*refs, count, places):
    *refs, index_ref = refs
    regroup(*refs, count=count, places=places)
    for k, ref in enumerate(refs[:count]):
        tile = ref[ref.shape[0] - INDEX_ROWS :, :]
        index_ref[k * INDEX_ROWS : (k + 1) * INDEX_ROWS, :] = tile.astype(jnp.float32).astype(jnp.int32)


def gather(me_ref, table, refs, by, near, place=0):
    others = table.shape[0] // len(refs)
    for i, ref in enumerate(refs):
        for n in range(others):
            table[natural(me_ref, i, n, by, near)] = ref[rows(place * others + n), :]


def spread(me_ref, table, refs, by, near):
    others = table.shape[0] // len(refs)
    for i, ref in enumerate(refs):
        for n in range(others):
            ref[rows(n), :] = table[natural(me_ref, i, n, by, near)].astype(ref.dtype)


def chosen_blocks(me_ref, index_ref, block, near, key_count):
    group = jnp.bitwise_xor(lax.rem(block, near), me_ref[0])
    row = group * INDEX_ROWS + lax.div(block, near)
    return [index_ref[row, j] for j in range(key_count)]


def pair_of(block_of, first, second):
    return jnp.concatenate(
        [jnp.concatenate([block_of(a), block_of(b)], axis=1) for a, b in zip(first, second, strict=True)], axis=0
    )


def set_diagonal(ref, first, second):
    ref[:BLK, :DH] = first
    ref[BLK:, DH:] = second


def add_pair(acc, chosen, values):
    for half, blocks in enumerate(chosen):
        for j, block in enumerate(blocks):
            acc[block] += values[j * BLK : (j + 1) * BLK, half * DH : (half + 1) * DH]


def for_pairs(me_ref, index_ref, count, near, key_count, unroll, one):
    def step(i, _):
        for slot in range(unroll):
            pair = i * unroll + slot
            blocks = (2 * pair, 2 * pair + 1)
            one(pair, slot, blocks, [chosen_blocks(me_ref, index_ref, b, near, key_count) for b in blocks])
        return 0

    lax.fori_loop(0, count // unroll, step, 0)


def joined_block(ref, blocks, place):
    arrays = ref.shape[0] // (blocks * BLK)
    return lambda b: ref[rows(b * arrays + place), :]


def softmax_weights(me_ref, index_ref, joined_ref, w_ref, half_ref, q_diag, *, parts, near, key_count, unroll):
    query, key = (joined_block(joined_ref, near * parts, place) for place in range(2))
    q_diag[...] = jnp.zeros_like(q_diag)

    def one(pair, slot, blocks, chosen):
        set_diagonal(q_diag.at[slot], *map(query, blocks))
        keys = pair_of(key, *chosen)
        scores = lax.dot_general(keys, q_diag[slot], NT, preferred_element_type=jnp.float32)
        row_max = jnp.max(scores, axis=0, keepdims=True)
        exp_scores = jnp.exp2((scores - row_max) * (SCALE * LOG2_E))
        weights = exp_scores * (1.0 / jnp.sum(exp_scores, axis=0, keepdims=True))
        w_ref[pair] = weights * SCALE
        half_ref[pair] = weights.astype(half_ref.dtype)

    for_pairs(me_ref, index_ref, w_ref.shape[0], near, key_count, unroll, one)


def dv_parts(me_ref, index_ref, half_ref, *refs, parts, near, key_count, unroll):
    g_refs, dv_refs, (acc, g_table, g_diag) = refs[:parts], refs[parts : 2 * parts], refs[2 * parts :]
    gather(me_ref, g_table, g_refs, "head", near)
    for ref in (acc, g_diag):
        ref[...] = jnp.zeros_like(ref)

    def one(pair, slot, blocks, chosen):
        set_diagonal(g_diag.at[slot], *(g_table[b] for b in blocks))
        add_pair(acc, chosen, jnp.dot(half_ref[pair], g_diag[slot], preferred_element_type=jnp.float32))

    for_pairs(me_ref, index_ref, half_ref.shape[0], near, key_count, unroll, one)
    spread(me_ref, acc, dv_refs, "head", near)


def dq_and_dk(me_ref, index_ref, joined_ref, *refs, parts, near, key_count, unroll):
    g_refs, v_refs, refs = refs[:parts], refs[parts : 2 * parts], refs[2 * parts :]
    w_ref, out_ref, acc, g_table, v_table, q_diag, g_diag = refs
    gather(me_ref, g_table, g_refs, "head", near)
    gather(me_ref, v_table, v_refs, "head", near)
    for ref in (acc, q_diag, g_diag):
        ref[...] = jnp.zeros_like(ref)
    query, key = (joined_block(joined_ref, near * parts, place) for place in range(2))

    def one(pair, slot, blocks, chosen):
        set_diagonal(q_diag.at[slot], *map(query, blocks))
        set_diagonal(g_diag.at[slot], *(g_table[b] for b in blocks))
        values = pair_of(lambda b: v_table[b], *chosen)
        prob_grad = lax.dot_general(values, g_diag[slot], NT, preferred_element_type=jnp.float32)
        scaled = w_ref[pair]
        row_delta = jnp.sum(scaled * prob_grad, axis=0, keepdims=True) * (1 / SCALE)
        score_grad = (scaled * (prob_grad - row_delta)).astype(jnp.bfloat16)
        add_pair(acc, chosen, jnp.dot(score_grad, q_diag[slot], preferred_element_type=jnp.float32))
        keys = pair_of(key, *chosen)
        grads = lax.dot_general(score_grad, keys, TN, preferred_element_type=jnp.float32)
        for half, block in enumerate(blocks):
            own = slice(half * BLK, (half + 1) * BLK)
            out_ref[rows(2 * block), :] = grads[own, own].astype(out_ref.dtype)

    for_pairs(me_ref, index_ref, w_ref.shape[0], near, key_count, unroll, one)
    for block in range(acc.shape[0]):
        out_ref[rows(2 * block + 1), :] = acc[block].astype(out_ref.dtype)


def whole_cluster(
    queries, key_vecs, value_vecs, out_grads, local_offsets, partner_pool, partner_picks
):
    bits = partner_pool.shape[1]
    parts = lax.axis_size("head")
    near = 1 << bits
    cluster = near * parts
    key_count = local_offsets.shape[1] + bits * partner_picks.shape[2]
    group = lax.axis_index("ctx")
    me = jnp.stack([jnp.bitwise_and(group, near - 1), lax.axis_index("head"), group]).astype(jnp.int32)

    def over_ctx(by_part):
        return [x if k == 0 else swapped(x, "ctx", k) for k, x in enumerate(by_part)]

    def over_head(by_part):
        return [x if j == 0 else swapped(x, "head", j) for j, x in enumerate(by_part)]

    members = [
        [member * parts + part for part in range(parts) for member in range(first, first + near)]
        for first in range(0, lax.axis_size("ctx"), near)
    ]
    exchange = functools.partial(
        lax.all_to_all, axis_name=("ctx", "head"), split_axis=0, concat_axis=0, tiled=True, axis_index_groups=members
    )
    joined = local_call(pack_natural, parts_of(2 * cluster, 1)[0], (), (queries, key_vecs))
    later = (out_grads, value_vecs, local_offsets, partner_pool, partner_picks)
    joined, later = lax.optimization_barrier((joined, later))
    out_grads, value_vecs, local_offsets, partner_pool, partner_picks = later
    joined = exchange(joined)
    grad = local_call(
        functools.partial(pack, arrays=1, others=parts, by="ctx", near=near), parts_of(parts, near), (me,), (out_grads,)
    )
    grad = local_call(functools.partial(regroup, count=near, places=[0]), parts_of(near, parts), (), over_ctx(grad))
    grad = over_head(grad)
    value = local_call(
        functools.partial(pack_with_index, arrays=1, others=parts, parts=parts, near=near),
        parts_of(parts, near, INDEX_ROWS),
        (me, local_offsets, partner_pool, partner_picks),
        (value_vecs,),
    )
    *value, index = local_call(
        functools.partial(regroup_with_index, count=near, places=[0]),
        parts_of(near, parts) + [jax.ShapeDtypeStruct((near * INDEX_ROWS, DH), jnp.int32)],
        (),
        over_ctx(value),
    )
    joined, value = lax.optimization_barrier((joined, value))
    value = over_head(value)

    pairs, keys = cluster // 2, key_count * BLK
    unroll = next(n for n in (8, 4, 2, 1) if pairs % n == 0)
    kwargs = dict(parts=parts, near=near, key_count=key_count, unroll=unroll)
    flops = 4 * cluster * keys * BLK * DH
    acc, table = (pltpu.VMEM((cluster, BLK, DH), dtype) for dtype in (jnp.float32, jnp.bfloat16))
    diagonal = pltpu.VMEM((unroll, 2 * BLK, 2 * DH), jnp.bfloat16)
    weights, half = local_call(
        functools.partial(softmax_weights, **kwargs),
        [jax.ShapeDtypeStruct((pairs, keys, 2 * BLK), dtype) for dtype in (jnp.float32, jnp.bfloat16)],
        (me, index),
        (joined,),
        [diagonal],
        flops // 2,
    )
    dv = local_call(
        functools.partial(dv_parts, **kwargs),
        parts_of(near, parts),
        (me, index),
        (half, *grad),
        [acc, table, diagonal],
        flops // 2,
    )
    dv = over_head(dv)
    joined = local_call(
        functools.partial(dq_and_dk, **kwargs),
        parts_of(2 * cluster, 1)[0],
        (me, index),
        (joined, *grad, *value, weights),
        [acc] + [table] * 2 + [diagonal] * 2,
        flops * 3 // 2,
    )
    joined, dv = lax.optimization_barrier((joined, dv))
    joined = exchange(joined)
    dv = local_call(functools.partial(regroup, count=parts, places=[0]), parts_of(parts, near), (), dv)
    dv = over_ctx(dv)
    out = jax.ShapeDtypeStruct(queries.shape, queries.dtype)
    value_grads = local_call(functools.partial(unpack, by="ctx", near=near), out, (me,), dv)
    query_grads, key_grads = local_call(unpack_natural, [out] * 2, (), (joined,))
    return query_grads, key_grads, value_grads


def attend_kernel(
    index_ref, q_ref, k_ref, v_ref, g_ref, dq_ref, dk_ref, dv_ref, acc_k, acc_v, k_turned, k_cat, v_cat, kt_cat
):
    query_blocks = q_ref.shape[0] // BLK
    table_blocks = k_ref.shape[0] // BLK
    key_count = k_cat.shape[0] // BLK

    acc_k[...] = jnp.zeros_like(acc_k)
    acc_v[...] = jnp.zeros_like(acc_v)
    for block in range(table_blocks):
        k_turned[block] = k_ref[block * BLK : (block + 1) * BLK, :].T

    def step(block, _):
        query = q_ref[rows(block), :]
        grad = g_ref[rows(block), :]
        chosen = [index_ref[block * key_count + j] for j in range(key_count)]
        for j in range(key_count):
            part = slice(j * BLK, (j + 1) * BLK)
            k_cat[part, :] = k_ref[rows(chosen[j]), :]
            v_cat[part, :] = v_ref[rows(chosen[j]), :]
            kt_cat[:, part] = k_turned[chosen[j]]
        scores = lax.dot_general(k_cat[...], query, NT, preferred_element_type=jnp.float32)
        row_max = jnp.max(scores, axis=0, keepdims=True)
        exp_scores = jnp.exp2((scores - row_max) * (SCALE * LOG2_E))
        weights = exp_scores * (1.0 / jnp.sum(exp_scores, axis=0, keepdims=True))
        prob_grad = lax.dot_general(v_cat[...], grad, NT, preferred_element_type=jnp.float32)
        row_delta = jnp.sum(weights * prob_grad, axis=0, keepdims=True)
        score_grad = (SCALE * weights * (prob_grad - row_delta)).astype(jnp.bfloat16)
        weights_half = weights.astype(jnp.bfloat16)
        query_turned = jnp.dot(kt_cat[...], score_grad, preferred_element_type=jnp.float32)
        dq_ref[rows(block), :] = query_turned.T.astype(jnp.bfloat16)
        key_out = jnp.dot(score_grad, query, preferred_element_type=jnp.float32)
        value_out = jnp.dot(weights_half, grad, preferred_element_type=jnp.float32)
        for j in range(key_count):
            part = slice(j * BLK, (j + 1) * BLK)
            acc_k[rows(chosen[j]), :] += key_out[part]
            acc_v[rows(chosen[j]), :] += value_out[part]
        return 0

    lax.fori_loop(0, query_blocks, step, 0)
    dk_ref[...] = acc_k[...].astype(dk_ref.dtype)
    dv_ref[...] = acc_v[...].astype(dv_ref.dtype)


def attend(index, query, key, value, grad, table_type):
    heads = query.shape[1] // DH
    key_count = index.shape[1]
    tokens, table = query.shape[0], key.shape[0]
    token_spec = pl.BlockSpec((tokens, DH), lambda h, *_: (0, h))
    table_spec = pl.BlockSpec((table, DH), lambda h, *_: (0, h))
    return pl.pallas_call(
        attend_kernel,
        grid_spec=pltpu.PrefetchScalarGridSpec(
            num_scalar_prefetch=1,
            grid=(heads,),
            in_specs=[token_spec, table_spec, table_spec, token_spec],
            out_specs=[token_spec, table_spec, table_spec],
            scratch_shapes=[
                pltpu.VMEM((table, DH), jnp.float32),
                pltpu.VMEM((table, DH), jnp.float32),
                pltpu.VMEM((table // BLK, DH, BLK), jnp.bfloat16),
                pltpu.VMEM((key_count * BLK, DH), jnp.bfloat16),
                pltpu.VMEM((key_count * BLK, DH), jnp.bfloat16),
                pltpu.VMEM((DH, key_count * BLK), jnp.bfloat16),
            ],
        ),
        out_shape=[
            jax.ShapeDtypeStruct(query.shape, jnp.bfloat16),
            jax.ShapeDtypeStruct(key.shape, table_type),
            jax.ShapeDtypeStruct(key.shape, table_type),
        ],
        compiler_params=pltpu.CompilerParams(vmem_limit_bytes=VMEM_BYTES),
        name="attend",
    )(index.reshape(-1), query, key, value, grad)


def by_pools(
    queries, key_vecs, value_vecs, out_grads, local_offsets, partner_pool, partner_picks
):
    to_heads = functools.partial(lax.all_to_all, axis_name="head", split_axis=1, concat_axis=0, tiled=True)
    to_tokens = functools.partial(lax.all_to_all, axis_name="head", split_axis=0, concat_axis=1, tiled=True)
    query, key, value, grad = (to_heads(x) for x in (queries, key_vecs, value_vecs, out_grads))
    width = query.shape[1]
    blocks = query.shape[0] // BLK
    bits, pool_size = partner_pool.shape[1:]
    group = lax.axis_index("ctx")
    asked = [partner_pool[jnp.bitwise_xor(group, 1 << bit), bit] for bit in range(bits)]

    def table(array):
        by_block = array.reshape(blocks, BLK, width)
        far = [swapped(by_block[asked[bit]], "ctx", 1 << bit) for bit in range(bits)]
        return jnp.concatenate([by_block] + far).reshape(-1, width)

    inner = jnp.arange(blocks, dtype=jnp.int32)
    own = (inner[:, None] + local_offsets) % blocks
    far = blocks + jnp.arange(bits, dtype=jnp.int32)[None, :, None] * pool_size + partner_picks
    index = jnp.concatenate([own, far.reshape(blocks, -1)], axis=1).astype(jnp.int32)
    dq, *tables = attend(index, query, table(key), table(value), grad, jnp.float32)
    grads = [dq]
    for array in tables:
        by_block = array.reshape(-1, BLK, width)
        total = by_block[:blocks]
        for bit in range(bits):
            lower = blocks + bit * pool_size
            back = swapped(by_block[lower : lower + pool_size], "ctx", 1 << bit)
            total = total.at[asked[bit]].add(back)
        grads.append(total.reshape(blocks * BLK, width).astype(jnp.bfloat16))
    return tuple(to_tokens(x) for x in grads)


def per_device(*args):
    tokens, features = args[0].shape
    parts = lax.axis_size("head")
    cluster = parts << args[5].shape[1]
    if features // DH == cluster and tokens == BLK and parts & (parts - 1) == 0 and 1 < parts <= INDEX_ROWS:
        return whole_cluster(*args)
    return by_pools(*args)


def solution(mesh):
    return jax.shard_map(
        per_device,
        mesh=mesh,
        in_specs=(
            P(("ctx", "head"), None),
            P(("ctx", "head"), None),
            P(("ctx", "head"), None),
            P(("ctx", "head"), None),
            P("ctx", None),
            P(),
            P("ctx", None, None),
        ),
        out_specs=(P(("ctx", "head"), None), P(("ctx", "head"), None), P(("ctx", "head"), None)),
        check_vma=False,
    )
```

```python
import functools

import jax
import jax.numpy as jnp
from jax import lax
from jax.experimental import pallas as pl
from jax.experimental.pallas import tpu as pltpu
from jax.sharding import PartitionSpec as P

DH = 128
BLK = 128
SCALE = DH**-0.5
LOG2_E = 1.4426950408889634
NT = (((1,), (1,)), ((), ()))
TN = (((0,), (0,)), ((), ()))
VMEM_BYTES = 16 << 20
IN_VMEM = pl.BlockSpec(memory_space=pltpu.VMEM)
IN_SMEM = pl.BlockSpec(memory_space=pltpu.SMEM)
IN_HBM = pl.BlockSpec(memory_space=pl.ANY)
INDEX_ROWS = 16


def swapped(value, axis, distance):
    return lax.ppermute(value, axis, [(i, i ^ distance) for i in range(lax.axis_size(axis))])


def rows(block):
    return pl.ds(block * BLK if isinstance(block, int) else pl.multiple_of(block * BLK, BLK), BLK)


def head_lanes(head):
    return pl.ds(pl.multiple_of(head * DH, DH), DH)


def local_call(kernel, out_shape, scalars, arrays, scratch=(), flops=0, arrays_in=IN_VMEM, vmem_bytes=VMEM_BYTES):
    moved = sum(x.size * x.dtype.itemsize for x in (*arrays, *jax.tree.leaves(out_shape)))
    return pl.pallas_call(
        kernel,
        out_shape=out_shape,
        in_specs=[IN_SMEM] * len(scalars) + [arrays_in] * len(arrays),
        out_specs=jax.tree.map(lambda _: IN_VMEM, out_shape),
        scratch_shapes=list(scratch),
        compiler_params=pltpu.CompilerParams(vmem_limit_bytes=vmem_bytes),
        cost_estimate=pl.CostEstimate(flops=flops, bytes_accessed=moved, transcendentals=0),
        name=getattr(kernel, "func", kernel).__name__,
    )(*scalars, *arrays)


def parts_of(blocks, count, extra=0):
    return [jax.ShapeDtypeStruct((blocks * BLK + extra, DH), jnp.bfloat16)] * count


def natural(me_ref, i, n, by, near):
    k, j = (i, n) if by == "ctx" else (n, i)
    return jnp.bitwise_xor(me_ref[1], j) * near + jnp.bitwise_xor(me_ref[0], k)


def pack(me_ref, *refs, arrays, others, by, near):
    ins, outs = refs[:arrays], refs[arrays:]
    for i, out in enumerate(outs):
        for n in range(others):
            lanes = head_lanes(natural(me_ref, i, n, by, near))
            for place, ref in enumerate(ins):
                out[rows(place * others + n), :] = ref[:, lanes]


def pack_with_index(me_ref, offsets_ref, pool_ref, picks_ref, *refs, parts, near, **kwargs):
    pack(me_ref, *refs, by="ctx", near=near, **kwargs)
    row = lax.broadcasted_iota(jnp.int32, (INDEX_ROWS, DH), 0)
    lane = lax.broadcasted_iota(jnp.int32, (INDEX_ROWS, DH), 1)
    tile = jnp.zeros((INDEX_ROWS, DH), jnp.int32)
    for block in range(parts):
        local = [offsets_ref[block, n] for n in range(offsets_ref.shape[1])]
        chosen = [jnp.bitwise_and(block + offset, parts - 1) * near + me_ref[0] for offset in local]
        for bit in range(picks_ref.shape[1]):
            far = jnp.bitwise_xor(me_ref[0], 1 << bit)
            for n in range(picks_ref.shape[2]):
                chosen.append(pool_ref[me_ref[2], bit, picks_ref[block, bit, n]] * near + far)
        for n, value in enumerate(chosen):
            tile = jnp.where((row == block) & (lane == n), value, tile)
    for out in refs[kwargs["arrays"] :]:
        out[out.shape[0] - INDEX_ROWS :, :] = tile.astype(jnp.float32).astype(out.dtype)


def unpack(me_ref, *refs, by, near):
    *ins, out = refs
    for i, ref in enumerate(ins):
        for n in range(ref.shape[0] // BLK):
            out[:, head_lanes(natural(me_ref, i, n, by, near))] = ref[rows(n), :]


def pack_natural(*refs):
    *ins, out, copied = refs
    copies = []
    for head in range(ins[0].shape[1] // DH):
        for place, ref in enumerate(ins):
            target = head * len(ins) + place
            source = ref.at[:, head * DH : (head + 1) * DH]
            copies.append(pltpu.make_async_copy(source, out.at[rows(target), :], copied.at[target]))
    for copy in copies:
        copy.start()
    for copy in copies:
        copy.wait()


def unpack_natural(ref, *outs):
    for head in range(outs[0].shape[1] // DH):
        for place, out in enumerate(outs):
            out[:, head * DH : (head + 1) * DH] = ref[rows(head * len(outs) + place), :]


def regroup(*refs, count, places):
    ins, outs = refs[:count], refs[count:]
    for i, out in enumerate(outs):
        for n, place in enumerate(places):
            for k, ref in enumerate(ins):
                out[rows(n * count + k), :] = ref[rows(place * len(outs) + i), :]


def regroup_with_index(*refs, count, places):
    *refs, index_ref = refs
    regroup(*refs, count=count, places=places)
    for k, ref in enumerate(refs[:count]):
        tile = ref[ref.shape[0] - INDEX_ROWS :, :]
        index_ref[k * INDEX_ROWS : (k + 1) * INDEX_ROWS, :] = tile.astype(jnp.float32).astype(jnp.int32)


def gather(me_ref, table, refs, by, near, place=0):
    others = table.shape[0] // len(refs)
    for i, ref in enumerate(refs):
        for n in range(others):
            table[natural(me_ref, i, n, by, near)] = ref[rows(place * others + n), :]


def spread(me_ref, table, refs, by, near):
    others = table.shape[0] // len(refs)
    for i, ref in enumerate(refs):
        for n in range(others):
            ref[rows(n), :] = table[natural(me_ref, i, n, by, near)].astype(ref.dtype)


def chosen_blocks(me_ref, index_ref, block, near, key_count):
    group = jnp.bitwise_xor(lax.rem(block, near), me_ref[0])
    row = group * INDEX_ROWS + lax.div(block, near)
    return [index_ref[row, j] for j in range(key_count)]


def pair_of(block_of, first, second):
    return jnp.concatenate(
        [jnp.concatenate([block_of(a), block_of(b)], axis=1) for a, b in zip(first, second, strict=True)], axis=0
    )


def set_diagonal(ref, first, second):
    ref[:BLK, :DH] = first
    ref[BLK:, DH:] = second


def add_pair(acc, chosen, values):
    for half, blocks in enumerate(chosen):
        for j, block in enumerate(blocks):
            acc[block] += values[j * BLK : (j + 1) * BLK, half * DH : (half + 1) * DH]


def for_pairs(me_ref, index_ref, count, near, key_count, unroll, one):
    def step(i, _):
        for slot in range(unroll):
            pair = i * unroll + slot
            blocks = (2 * pair, 2 * pair + 1)
            one(pair, slot, blocks, [chosen_blocks(me_ref, index_ref, b, near, key_count) for b in blocks])
        return 0

    lax.fori_loop(0, count // unroll, step, 0)


def joined_block(ref, blocks, place):
    arrays = ref.shape[0] // (blocks * BLK)
    return lambda b: ref[rows(b * arrays + place), :]


def softmax_weights(me_ref, index_ref, joined_ref, w_ref, half_ref, q_diag, *, parts, near, key_count, unroll):
    query, key = (joined_block(joined_ref, near * parts, place) for place in range(2))
    q_diag[...] = jnp.zeros_like(q_diag)

    def one(pair, slot, blocks, chosen):
        set_diagonal(q_diag.at[slot], *map(query, blocks))
        keys = pair_of(key, *chosen)
        scores = lax.dot_general(keys, q_diag[slot], NT, preferred_element_type=jnp.float32)
        row_max = jnp.max(scores, axis=0, keepdims=True)
        exp_scores = jnp.exp2((scores - row_max) * (SCALE * LOG2_E))
        weights = exp_scores * (1.0 / jnp.sum(exp_scores, axis=0, keepdims=True))
        w_ref[pair] = weights * SCALE
        half_ref[pair] = weights.astype(half_ref.dtype)

    for_pairs(me_ref, index_ref, w_ref.shape[0], near, key_count, unroll, one)


def dv_parts(me_ref, index_ref, half_ref, *refs, parts, near, key_count, unroll):
    g_refs, dv_refs, (acc, g_table, g_diag) = refs[:parts], refs[parts : 2 * parts], refs[2 * parts :]
    gather(me_ref, g_table, g_refs, "head", near)
    for ref in (acc, g_diag):
        ref[...] = jnp.zeros_like(ref)

    def one(pair, slot, blocks, chosen):
        set_diagonal(g_diag.at[slot], *(g_table[b] for b in blocks))
        add_pair(acc, chosen, jnp.dot(half_ref[pair], g_diag[slot], preferred_element_type=jnp.float32))

    for_pairs(me_ref, index_ref, half_ref.shape[0], near, key_count, unroll, one)
    spread(me_ref, acc, dv_refs, "head", near)


def dq_and_dk(me_ref, index_ref, joined_ref, *refs, parts, near, key_count, unroll):
    g_refs, v_refs, refs = refs[:parts], refs[parts : 2 * parts], refs[2 * parts :]
    w_ref, out_ref, acc, g_table, v_table, q_diag, g_diag = refs
    gather(me_ref, g_table, g_refs, "head", near)
    gather(me_ref, v_table, v_refs, "head", near)
    for ref in (acc, q_diag, g_diag):
        ref[...] = jnp.zeros_like(ref)
    query, key = (joined_block(joined_ref, near * parts, place) for place in range(2))

    def one(pair, slot, blocks, chosen):
        set_diagonal(q_diag.at[slot], *map(query, blocks))
        set_diagonal(g_diag.at[slot], *(g_table[b] for b in blocks))
        values = pair_of(lambda b: v_table[b], *chosen)
        prob_grad = lax.dot_general(values, g_diag[slot], NT, preferred_element_type=jnp.float32)
        scaled = w_ref[pair]
        row_delta = jnp.sum(scaled * prob_grad, axis=0, keepdims=True) * (1 / SCALE)
        score_grad = (scaled * (prob_grad - row_delta)).astype(jnp.bfloat16)
        add_pair(acc, chosen, jnp.dot(score_grad, q_diag[slot], preferred_element_type=jnp.float32))
        keys = pair_of(key, *chosen)
        grads = lax.dot_general(score_grad, keys, TN, preferred_element_type=jnp.float32)
        for half, block in enumerate(blocks):
            own = slice(half * BLK, (half + 1) * BLK)
            out_ref[rows(2 * block), :] = grads[own, own].astype(out_ref.dtype)

    for_pairs(me_ref, index_ref, w_ref.shape[0], near, key_count, unroll, one)
    for block in range(acc.shape[0]):
        out_ref[rows(2 * block + 1), :] = acc[block].astype(out_ref.dtype)


def whole_cluster(
    queries, key_vecs, value_vecs, out_grads, local_offsets, partner_pool, partner_picks
):
    bits = partner_pool.shape[1]
    parts = lax.axis_size("head")
    near = 1 << bits
    cluster = near * parts
    key_count = local_offsets.shape[1] + bits * partner_picks.shape[2]
    group = lax.axis_index("ctx")
    me = jnp.stack([jnp.bitwise_and(group, near - 1), lax.axis_index("head"), group]).astype(jnp.int32)

    def over_ctx(by_part):
        return [x if k == 0 else swapped(x, "ctx", k) for k, x in enumerate(by_part)]

    def over_head(by_part):
        return [x if j == 0 else swapped(x, "head", j) for j, x in enumerate(by_part)]

    members = [
        [member * parts + part for part in range(parts) for member in range(first, first + near)]
        for first in range(0, lax.axis_size("ctx"), near)
    ]
    exchange = functools.partial(
        lax.all_to_all, axis_name=("ctx", "head"), split_axis=0, concat_axis=0, tiled=True, axis_index_groups=members
    )
    joined = local_call(
        pack_natural,
        parts_of(2 * cluster, 1)[0],
        (),
        (queries, key_vecs),
        [pltpu.SemaphoreType.DMA((2 * cluster,))],
        arrays_in=IN_HBM,
        vmem_bytes=58 << 20,
    )
    later = (out_grads, value_vecs, local_offsets, partner_pool, partner_picks)
    joined, later = lax.optimization_barrier((joined, later))
    out_grads, value_vecs, local_offsets, partner_pool, partner_picks = later
    joined = exchange(joined)
    grad = local_call(
        functools.partial(pack, arrays=1, others=parts, by="ctx", near=near), parts_of(parts, near), (me,), (out_grads,)
    )
    grad = local_call(functools.partial(regroup, count=near, places=[0]), parts_of(near, parts), (), over_ctx(grad))
    grad = over_head(grad)
    value = local_call(
        functools.partial(pack_with_index, arrays=1, others=parts, parts=parts, near=near),
        parts_of(parts, near, INDEX_ROWS),
        (me, local_offsets, partner_pool, partner_picks),
        (value_vecs,),
    )
    *value, index = local_call(
        functools.partial(regroup_with_index, count=near, places=[0]),
        parts_of(near, parts) + [jax.ShapeDtypeStruct((near * INDEX_ROWS, DH), jnp.int32)],
        (),
        over_ctx(value),
    )
    joined, value = lax.optimization_barrier((joined, value))
    middle, last = parts // 2, parts - 1
    value[middle], grad[last] = lax.optimization_barrier((value[middle], grad[last]))
    value = over_head(value)

    pairs, keys = cluster // 2, key_count * BLK
    unroll = next(n for n in (8, 4, 2, 1) if pairs % n == 0)
    kwargs = dict(parts=parts, near=near, key_count=key_count, unroll=unroll)
    flops = 4 * cluster * keys * BLK * DH
    acc, table = (pltpu.VMEM((cluster, BLK, DH), dtype) for dtype in (jnp.float32, jnp.bfloat16))
    diagonal = pltpu.VMEM((unroll, 2 * BLK, 2 * DH), jnp.bfloat16)
    weights, half = local_call(
        functools.partial(softmax_weights, **kwargs),
        [jax.ShapeDtypeStruct((pairs, keys, 2 * BLK), dtype) for dtype in (jnp.float32, jnp.bfloat16)],
        (me, index),
        (joined,),
        [diagonal],
        flops // 2,
    )
    dv = local_call(
        functools.partial(dv_parts, **kwargs),
        parts_of(near, parts),
        (me, index),
        (half, *grad),
        [acc, table, diagonal],
        flops // 2,
    )
    dv = over_head(dv)
    joined = local_call(
        functools.partial(dq_and_dk, **kwargs),
        parts_of(2 * cluster, 1)[0],
        (me, index),
        (joined, *grad, *value, weights),
        [acc] + [table] * 2 + [diagonal] * 2,
        flops * 3 // 2,
    )
    joined, dv = lax.optimization_barrier((joined, dv))
    joined = exchange(joined)
    dv = local_call(functools.partial(regroup, count=parts, places=[0]), parts_of(parts, near), (), dv)
    dv = over_ctx(dv)
    out = jax.ShapeDtypeStruct(queries.shape, queries.dtype)
    value_grads = local_call(functools.partial(unpack, by="ctx", near=near), out, (me,), dv)
    query_grads, key_grads = local_call(unpack_natural, [out] * 2, (), (joined,))
    return query_grads, key_grads, value_grads


def attend_kernel(
    index_ref, q_ref, k_ref, v_ref, g_ref, dq_ref, dk_ref, dv_ref, acc_k, acc_v, k_turned, k_cat, v_cat, kt_cat
):
    query_blocks = q_ref.shape[0] // BLK
    table_blocks = k_ref.shape[0] // BLK
    key_count = k_cat.shape[0] // BLK

    acc_k[...] = jnp.zeros_like(acc_k)
    acc_v[...] = jnp.zeros_like(acc_v)
    for block in range(table_blocks):
        k_turned[block] = k_ref[block * BLK : (block + 1) * BLK, :].T

    def step(block, _):
        query = q_ref[rows(block), :]
        grad = g_ref[rows(block), :]
        chosen = [index_ref[block * key_count + j] for j in range(key_count)]
        for j in range(key_count):
            part = slice(j * BLK, (j + 1) * BLK)
            k_cat[part, :] = k_ref[rows(chosen[j]), :]
            v_cat[part, :] = v_ref[rows(chosen[j]), :]
            kt_cat[:, part] = k_turned[chosen[j]]
        scores = lax.dot_general(k_cat[...], query, NT, preferred_element_type=jnp.float32)
        row_max = jnp.max(scores, axis=0, keepdims=True)
        exp_scores = jnp.exp2((scores - row_max) * (SCALE * LOG2_E))
        weights = exp_scores * (1.0 / jnp.sum(exp_scores, axis=0, keepdims=True))
        prob_grad = lax.dot_general(v_cat[...], grad, NT, preferred_element_type=jnp.float32)
        row_delta = jnp.sum(weights * prob_grad, axis=0, keepdims=True)
        score_grad = (SCALE * weights * (prob_grad - row_delta)).astype(jnp.bfloat16)
        weights_half = weights.astype(jnp.bfloat16)
        query_turned = jnp.dot(kt_cat[...], score_grad, preferred_element_type=jnp.float32)
        dq_ref[rows(block), :] = query_turned.T.astype(jnp.bfloat16)
        key_out = jnp.dot(score_grad, query, preferred_element_type=jnp.float32)
        value_out = jnp.dot(weights_half, grad, preferred_element_type=jnp.float32)
        for j in range(key_count):
            part = slice(j * BLK, (j + 1) * BLK)
            acc_k[rows(chosen[j]), :] += key_out[part]
            acc_v[rows(chosen[j]), :] += value_out[part]
        return 0

    lax.fori_loop(0, query_blocks, step, 0)
    dk_ref[...] = acc_k[...].astype(dk_ref.dtype)
    dv_ref[...] = acc_v[...].astype(dv_ref.dtype)


def attend(index, query, key, value, grad, table_type):
    heads = query.shape[1] // DH
    key_count = index.shape[1]
    tokens, table = query.shape[0], key.shape[0]
    token_spec = pl.BlockSpec((tokens, DH), lambda h, *_: (0, h))
    table_spec = pl.BlockSpec((table, DH), lambda h, *_: (0, h))
    return pl.pallas_call(
        attend_kernel,
        grid_spec=pltpu.PrefetchScalarGridSpec(
            num_scalar_prefetch=1,
            grid=(heads,),
            in_specs=[token_spec, table_spec, table_spec, token_spec],
            out_specs=[token_spec, table_spec, table_spec],
            scratch_shapes=[
                pltpu.VMEM((table, DH), jnp.float32),
                pltpu.VMEM((table, DH), jnp.float32),
                pltpu.VMEM((table // BLK, DH, BLK), jnp.bfloat16),
                pltpu.VMEM((key_count * BLK, DH), jnp.bfloat16),
                pltpu.VMEM((key_count * BLK, DH), jnp.bfloat16),
                pltpu.VMEM((DH, key_count * BLK), jnp.bfloat16),
            ],
        ),
        out_shape=[
            jax.ShapeDtypeStruct(query.shape, jnp.bfloat16),
            jax.ShapeDtypeStruct(key.shape, table_type),
            jax.ShapeDtypeStruct(key.shape, table_type),
        ],
        compiler_params=pltpu.CompilerParams(vmem_limit_bytes=VMEM_BYTES),
        name="attend",
    )(index.reshape(-1), query, key, value, grad)


def by_pools(
    queries, key_vecs, value_vecs, out_grads, local_offsets, partner_pool, partner_picks
):
    to_heads = functools.partial(lax.all_to_all, axis_name="head", split_axis=1, concat_axis=0, tiled=True)
    to_tokens = functools.partial(lax.all_to_all, axis_name="head", split_axis=0, concat_axis=1, tiled=True)
    query, key, value, grad = (to_heads(x) for x in (queries, key_vecs, value_vecs, out_grads))
    width = query.shape[1]
    blocks = query.shape[0] // BLK
    bits, pool_size = partner_pool.shape[1:]
    group = lax.axis_index("ctx")
    asked = [partner_pool[jnp.bitwise_xor(group, 1 << bit), bit] for bit in range(bits)]

    def table(array):
        by_block = array.reshape(blocks, BLK, width)
        far = [swapped(by_block[asked[bit]], "ctx", 1 << bit) for bit in range(bits)]
        return jnp.concatenate([by_block] + far).reshape(-1, width)

    inner = jnp.arange(blocks, dtype=jnp.int32)
    own = (inner[:, None] + local_offsets) % blocks
    far = blocks + jnp.arange(bits, dtype=jnp.int32)[None, :, None] * pool_size + partner_picks
    index = jnp.concatenate([own, far.reshape(blocks, -1)], axis=1).astype(jnp.int32)
    dq, *tables = attend(index, query, table(key), table(value), grad, jnp.float32)
    grads = [dq]
    for array in tables:
        by_block = array.reshape(-1, BLK, width)
        total = by_block[:blocks]
        for bit in range(bits):
            lower = blocks + bit * pool_size
            back = swapped(by_block[lower : lower + pool_size], "ctx", 1 << bit)
            total = total.at[asked[bit]].add(back)
        grads.append(total.reshape(blocks * BLK, width).astype(jnp.bfloat16))
    return tuple(to_tokens(x) for x in grads)


def per_device(*args):
    tokens, features = args[0].shape
    parts = lax.axis_size("head")
    cluster = parts << args[5].shape[1]
    if features // DH == cluster and tokens == BLK and parts & (parts - 1) == 0 and 1 < parts <= INDEX_ROWS:
        return whole_cluster(*args)
    return by_pools(*args)


def solution(mesh):
    return jax.shard_map(
        per_device,
        mesh=mesh,
        in_specs=(
            P(("ctx", "head"), None),
            P(("ctx", "head"), None),
            P(("ctx", "head"), None),
            P(("ctx", "head"), None),
            P("ctx", None),
            P(),
            P("ctx", None, None),
        ),
        out_specs=(P(("ctx", "head"), None), P(("ctx", "head"), None), P(("ctx", "head"), None)),
        check_vma=False,
    )
```

```python
import functools

import jax
import jax.numpy as jnp
from jax import lax
from jax.experimental import pallas as pl
from jax.experimental.pallas import tpu as pltpu
from jax.sharding import PartitionSpec as P

DH = 128
BLK = 128
SCALE = DH**-0.5
LOG2_E = 1.4426950408889634
NT = (((1,), (1,)), ((), ()))
TN = (((0,), (0,)), ((), ()))
VMEM_BYTES = 16 << 20
IN_VMEM = pl.BlockSpec(memory_space=pltpu.VMEM)
IN_SMEM = pl.BlockSpec(memory_space=pltpu.SMEM)
IN_HBM = pl.BlockSpec(memory_space=pl.ANY)
INDEX_ROWS = 16


def swapped(value, axis, distance):
    return lax.ppermute(value, axis, [(i, i ^ distance) for i in range(lax.axis_size(axis))])


def rows(block):
    return pl.ds(block * BLK if isinstance(block, int) else pl.multiple_of(block * BLK, BLK), BLK)


def head_lanes(head):
    return pl.ds(pl.multiple_of(head * DH, DH), DH)


def local_call(kernel, out_shape, scalars, arrays, scratch=(), flops=0, arrays_in=IN_VMEM, outs_in=IN_VMEM, vmem_bytes=VMEM_BYTES):
    moved = sum(x.size * x.dtype.itemsize for x in (*arrays, *jax.tree.leaves(out_shape)))
    return pl.pallas_call(
        kernel,
        out_shape=out_shape,
        in_specs=[IN_SMEM] * len(scalars) + [arrays_in] * len(arrays),
        out_specs=jax.tree.map(lambda _: outs_in, out_shape),
        scratch_shapes=list(scratch),
        compiler_params=pltpu.CompilerParams(vmem_limit_bytes=vmem_bytes),
        cost_estimate=pl.CostEstimate(flops=flops, bytes_accessed=moved, transcendentals=0),
        name=getattr(kernel, "func", kernel).__name__,
    )(*scalars, *arrays)


def parts_of(blocks, count, extra=0):
    return [jax.ShapeDtypeStruct((blocks * BLK + extra, DH), jnp.bfloat16)] * count


def natural(me_ref, i, n, by, near):
    k, j = (i, n) if by == "ctx" else (n, i)
    return jnp.bitwise_xor(me_ref[1], j) * near + jnp.bitwise_xor(me_ref[0], k)


def pack(me_ref, *refs, arrays, others, by, near):
    ins, outs = refs[:arrays], refs[arrays:]
    for i, out in enumerate(outs):
        for n in range(others):
            lanes = head_lanes(natural(me_ref, i, n, by, near))
            for place, ref in enumerate(ins):
                out[rows(place * others + n), :] = ref[:, lanes]


def pack_with_index(me_ref, offsets_ref, pool_ref, picks_ref, *refs, parts, near, **kwargs):
    pack(me_ref, *refs, by="ctx", near=near, **kwargs)
    row = lax.broadcasted_iota(jnp.int32, (INDEX_ROWS, DH), 0)
    lane = lax.broadcasted_iota(jnp.int32, (INDEX_ROWS, DH), 1)
    tile = jnp.zeros((INDEX_ROWS, DH), jnp.int32)
    for block in range(parts):
        local = [offsets_ref[block, n] for n in range(offsets_ref.shape[1])]
        chosen = [jnp.bitwise_and(block + offset, parts - 1) * near + me_ref[0] for offset in local]
        for bit in range(picks_ref.shape[1]):
            far = jnp.bitwise_xor(me_ref[0], 1 << bit)
            for n in range(picks_ref.shape[2]):
                chosen.append(pool_ref[me_ref[2], bit, picks_ref[block, bit, n]] * near + far)
        for n, value in enumerate(chosen):
            tile = jnp.where((row == block) & (lane == n), value, tile)
    for out in refs[kwargs["arrays"] :]:
        out[out.shape[0] - INDEX_ROWS :, :] = tile.astype(jnp.float32).astype(out.dtype)


def unpack(me_ref, *refs, by, near):
    *ins, out = refs
    for i, ref in enumerate(ins):
        for n in range(ref.shape[0] // BLK):
            out[:, head_lanes(natural(me_ref, i, n, by, near))] = ref[rows(n), :]


def pack_natural(*refs):
    *ins, out, copied = refs
    copies = []
    for head in range(ins[0].shape[1] // DH):
        for place, ref in enumerate(ins):
            target = head * len(ins) + place
            source = ref.at[:, head * DH : (head + 1) * DH]
            copies.append(pltpu.make_async_copy(source, out.at[rows(target), :], copied.at[target]))
    for copy in copies:
        copy.start()
    for copy in copies:
        copy.wait()


def unpack_natural(ref, *refs):
    *outs, copied = refs
    copies = []
    for head in range(outs[0].shape[1] // DH):
        for place, out in enumerate(outs):
            source = head * len(outs) + place
            target = out.at[:, head * DH : (head + 1) * DH]
            copies.append(pltpu.make_async_copy(ref.at[rows(source), :], target, copied.at[source]))
    for copy in copies:
        copy.start()
    for copy in copies:
        copy.wait()


def regroup(*refs, count, places):
    ins, outs = refs[:count], refs[count:]
    for i, out in enumerate(outs):
        for n, place in enumerate(places):
            for k, ref in enumerate(ins):
                out[rows(n * count + k), :] = ref[rows(place * len(outs) + i), :]


def regroup_with_index(*refs, count, places):
    *refs, index_ref = refs
    regroup(*refs, count=count, places=places)
    for k, ref in enumerate(refs[:count]):
        tile = ref[ref.shape[0] - INDEX_ROWS :, :]
        index_ref[k * INDEX_ROWS : (k + 1) * INDEX_ROWS, :] = tile.astype(jnp.float32).astype(jnp.int32)


def gather(me_ref, table, refs, by, near, place=0):
    others = table.shape[0] // len(refs)
    for i, ref in enumerate(refs):
        for n in range(others):
            table[natural(me_ref, i, n, by, near)] = ref[rows(place * others + n), :]


def spread(me_ref, table, refs, by, near):
    others = table.shape[0] // len(refs)
    for i, ref in enumerate(refs):
        for n in range(others):
            ref[rows(n), :] = table[natural(me_ref, i, n, by, near)].astype(ref.dtype)


def chosen_blocks(me_ref, index_ref, block, near, key_count):
    group = jnp.bitwise_xor(lax.rem(block, near), me_ref[0])
    row = group * INDEX_ROWS + lax.div(block, near)
    return [index_ref[row, j] for j in range(key_count)]


def pair_of(block_of, first, second):
    return jnp.concatenate(
        [jnp.concatenate([block_of(a), block_of(b)], axis=1) for a, b in zip(first, second, strict=True)], axis=0
    )


def set_diagonal(ref, first, second):
    ref[:BLK, :DH] = first
    ref[BLK:, DH:] = second


def add_pair(acc, chosen, values):
    for half, blocks in enumerate(chosen):
        for j, block in enumerate(blocks):
            acc[block] += values[j * BLK : (j + 1) * BLK, half * DH : (half + 1) * DH]


def for_pairs(me_ref, index_ref, count, near, key_count, unroll, one):
    def step(i, _):
        for slot in range(unroll):
            pair = i * unroll + slot
            blocks = (2 * pair, 2 * pair + 1)
            one(pair, slot, blocks, [chosen_blocks(me_ref, index_ref, b, near, key_count) for b in blocks])
        return 0

    lax.fori_loop(0, count // unroll, step, 0)


def joined_block(ref, blocks, place):
    arrays = ref.shape[0] // (blocks * BLK)
    return lambda b: ref[rows(b * arrays + place), :]


def softmax_weights(me_ref, index_ref, joined_ref, w_ref, half_ref, q_diag, *, parts, near, key_count, unroll):
    query, key = (joined_block(joined_ref, near * parts, place) for place in range(2))
    q_diag[...] = jnp.zeros_like(q_diag)

    def one(pair, slot, blocks, chosen):
        set_diagonal(q_diag.at[slot], *map(query, blocks))
        keys = pair_of(key, *chosen)
        scores = lax.dot_general(keys, q_diag[slot], NT, preferred_element_type=jnp.float32)
        row_max = jnp.max(scores, axis=0, keepdims=True)
        exp_scores = jnp.exp2((scores - row_max) * (SCALE * LOG2_E))
        weights = exp_scores * (1.0 / jnp.sum(exp_scores, axis=0, keepdims=True))
        w_ref[pair] = weights * SCALE
        half_ref[pair] = weights.astype(half_ref.dtype)

    for_pairs(me_ref, index_ref, w_ref.shape[0], near, key_count, unroll, one)


def dv_parts(me_ref, index_ref, half_ref, *refs, parts, near, key_count, unroll):
    g_refs, dv_refs, (acc, g_table, g_diag) = refs[:parts], refs[parts : 2 * parts], refs[2 * parts :]
    gather(me_ref, g_table, g_refs, "head", near)
    for ref in (acc, g_diag):
        ref[...] = jnp.zeros_like(ref)

    def one(pair, slot, blocks, chosen):
        set_diagonal(g_diag.at[slot], *(g_table[b] for b in blocks))
        add_pair(acc, chosen, jnp.dot(half_ref[pair], g_diag[slot], preferred_element_type=jnp.float32))

    for_pairs(me_ref, index_ref, half_ref.shape[0], near, key_count, unroll, one)
    spread(me_ref, acc, dv_refs, "head", near)


def dq_and_dk(me_ref, index_ref, joined_ref, *refs, parts, near, key_count, unroll):
    g_refs, v_refs, refs = refs[:parts], refs[parts : 2 * parts], refs[2 * parts :]
    w_ref, out_ref, acc, g_table, v_table, q_diag, g_diag = refs
    gather(me_ref, g_table, g_refs, "head", near)
    gather(me_ref, v_table, v_refs, "head", near)
    for ref in (acc, q_diag, g_diag):
        ref[...] = jnp.zeros_like(ref)
    query, key = (joined_block(joined_ref, near * parts, place) for place in range(2))

    def one(pair, slot, blocks, chosen):
        set_diagonal(q_diag.at[slot], *map(query, blocks))
        set_diagonal(g_diag.at[slot], *(g_table[b] for b in blocks))
        values = pair_of(lambda b: v_table[b], *chosen)
        prob_grad = lax.dot_general(values, g_diag[slot], NT, preferred_element_type=jnp.float32)
        scaled = w_ref[pair]
        row_delta = jnp.sum(scaled * prob_grad, axis=0, keepdims=True) * (1 / SCALE)
        score_grad = (scaled * (prob_grad - row_delta)).astype(jnp.bfloat16)
        add_pair(acc, chosen, jnp.dot(score_grad, q_diag[slot], preferred_element_type=jnp.float32))
        keys = pair_of(key, *chosen)
        grads = lax.dot_general(score_grad, keys, TN, preferred_element_type=jnp.float32)
        for half, block in enumerate(blocks):
            own = slice(half * BLK, (half + 1) * BLK)
            out_ref[rows(2 * block), :] = grads[own, own].astype(out_ref.dtype)

    for_pairs(me_ref, index_ref, w_ref.shape[0], near, key_count, unroll, one)
    for block in range(acc.shape[0]):
        out_ref[rows(2 * block + 1), :] = acc[block].astype(out_ref.dtype)


def whole_cluster(
    queries, key_vecs, value_vecs, out_grads, local_offsets, partner_pool, partner_picks
):
    bits = partner_pool.shape[1]
    parts = lax.axis_size("head")
    near = 1 << bits
    cluster = near * parts
    key_count = local_offsets.shape[1] + bits * partner_picks.shape[2]
    group = lax.axis_index("ctx")
    me = jnp.stack([jnp.bitwise_and(group, near - 1), lax.axis_index("head"), group]).astype(jnp.int32)

    def over_ctx(by_part):
        return [x if k == 0 else swapped(x, "ctx", k) for k, x in enumerate(by_part)]

    def over_head(by_part):
        return [x if j == 0 else swapped(x, "head", j) for j, x in enumerate(by_part)]

    members = [
        [member * parts + part for part in range(parts) for member in range(first, first + near)]
        for first in range(0, lax.axis_size("ctx"), near)
    ]
    exchange = functools.partial(
        lax.all_to_all, axis_name=("ctx", "head"), split_axis=0, concat_axis=0, tiled=True, axis_index_groups=members
    )
    joined = local_call(
        pack_natural,
        parts_of(2 * cluster, 1)[0],
        (),
        (queries, key_vecs),
        [pltpu.SemaphoreType.DMA((2 * cluster,))],
        arrays_in=IN_HBM,
        vmem_bytes=58 << 20,
    )
    later = (out_grads, value_vecs, local_offsets, partner_pool, partner_picks)
    joined, later = lax.optimization_barrier((joined, later))
    out_grads, value_vecs, local_offsets, partner_pool, partner_picks = later
    joined = exchange(joined)
    grad = local_call(
        functools.partial(pack, arrays=1, others=parts, by="ctx", near=near), parts_of(parts, near), (me,), (out_grads,)
    )
    grad = local_call(functools.partial(regroup, count=near, places=[0]), parts_of(near, parts), (), over_ctx(grad))
    grad = over_head(grad)
    value = local_call(
        functools.partial(pack_with_index, arrays=1, others=parts, parts=parts, near=near),
        parts_of(parts, near, INDEX_ROWS),
        (me, local_offsets, partner_pool, partner_picks),
        (value_vecs,),
    )
    *value, index = local_call(
        functools.partial(regroup_with_index, count=near, places=[0]),
        parts_of(near, parts) + [jax.ShapeDtypeStruct((near * INDEX_ROWS, DH), jnp.int32)],
        (),
        over_ctx(value),
    )
    joined, value = lax.optimization_barrier((joined, value))
    middle, last = parts // 2, parts - 1
    value[middle], grad[last] = lax.optimization_barrier((value[middle], grad[last]))
    value = over_head(value)

    pairs, keys = cluster // 2, key_count * BLK
    unroll = next(n for n in (8, 4, 2, 1) if pairs % n == 0)
    kwargs = dict(parts=parts, near=near, key_count=key_count, unroll=unroll)
    flops = 4 * cluster * keys * BLK * DH
    acc, table = (pltpu.VMEM((cluster, BLK, DH), dtype) for dtype in (jnp.float32, jnp.bfloat16))
    diagonal = pltpu.VMEM((unroll, 2 * BLK, 2 * DH), jnp.bfloat16)
    weights, half = local_call(
        functools.partial(softmax_weights, **kwargs),
        [jax.ShapeDtypeStruct((pairs, keys, 2 * BLK), dtype) for dtype in (jnp.float32, jnp.bfloat16)],
        (me, index),
        (joined,),
        [diagonal],
        flops // 2,
    )
    dv = local_call(
        functools.partial(dv_parts, **kwargs),
        parts_of(near, parts),
        (me, index),
        (half, *grad),
        [acc, table, diagonal],
        flops // 2,
    )
    dv = over_head(dv)
    joined = local_call(
        functools.partial(dq_and_dk, **kwargs),
        parts_of(2 * cluster, 1)[0],
        (me, index),
        (joined, *grad, *value, weights),
        [acc] + [table] * 2 + [diagonal] * 2,
        flops * 3 // 2,
    )
    joined, dv = lax.optimization_barrier((joined, dv))
    joined = exchange(joined)
    dv = local_call(functools.partial(regroup, count=parts, places=[0]), parts_of(parts, near), (), dv)
    dv = over_ctx(dv)
    out = jax.ShapeDtypeStruct(queries.shape, queries.dtype)
    value_grads = local_call(functools.partial(unpack, by="ctx", near=near), out, (me,), dv)
    query_grads, key_grads = local_call(
        unpack_natural, [out] * 2, (), (joined,), [pltpu.SemaphoreType.DMA((2 * cluster,))], outs_in=IN_HBM
    )
    return query_grads, key_grads, value_grads


def attend_kernel(
    index_ref, q_ref, k_ref, v_ref, g_ref, dq_ref, dk_ref, dv_ref, acc_k, acc_v, k_turned, k_cat, v_cat, kt_cat
):
    query_blocks = q_ref.shape[0] // BLK
    table_blocks = k_ref.shape[0] // BLK
    key_count = k_cat.shape[0] // BLK

    acc_k[...] = jnp.zeros_like(acc_k)
    acc_v[...] = jnp.zeros_like(acc_v)
    for block in range(table_blocks):
        k_turned[block] = k_ref[block * BLK : (block + 1) * BLK, :].T

    def step(block, _):
        query = q_ref[rows(block), :]
        grad = g_ref[rows(block), :]
        chosen = [index_ref[block * key_count + j] for j in range(key_count)]
        for j in range(key_count):
            part = slice(j * BLK, (j + 1) * BLK)
            k_cat[part, :] = k_ref[rows(chosen[j]), :]
            v_cat[part, :] = v_ref[rows(chosen[j]), :]
            kt_cat[:, part] = k_turned[chosen[j]]
        scores = lax.dot_general(k_cat[...], query, NT, preferred_element_type=jnp.float32)
        row_max = jnp.max(scores, axis=0, keepdims=True)
        exp_scores = jnp.exp2((scores - row_max) * (SCALE * LOG2_E))
        weights = exp_scores * (1.0 / jnp.sum(exp_scores, axis=0, keepdims=True))
        prob_grad = lax.dot_general(v_cat[...], grad, NT, preferred_element_type=jnp.float32)
        row_delta = jnp.sum(weights * prob_grad, axis=0, keepdims=True)
        score_grad = (SCALE * weights * (prob_grad - row_delta)).astype(jnp.bfloat16)
        weights_half = weights.astype(jnp.bfloat16)
        query_turned = jnp.dot(kt_cat[...], score_grad, preferred_element_type=jnp.float32)
        dq_ref[rows(block), :] = query_turned.T.astype(jnp.bfloat16)
        key_out = jnp.dot(score_grad, query, preferred_element_type=jnp.float32)
        value_out = jnp.dot(weights_half, grad, preferred_element_type=jnp.float32)
        for j in range(key_count):
            part = slice(j * BLK, (j + 1) * BLK)
            acc_k[rows(chosen[j]), :] += key_out[part]
            acc_v[rows(chosen[j]), :] += value_out[part]
        return 0

    lax.fori_loop(0, query_blocks, step, 0)
    dk_ref[...] = acc_k[...].astype(dk_ref.dtype)
    dv_ref[...] = acc_v[...].astype(dv_ref.dtype)


def attend(index, query, key, value, grad, table_type):
    heads = query.shape[1] // DH
    key_count = index.shape[1]
    tokens, table = query.shape[0], key.shape[0]
    token_spec = pl.BlockSpec((tokens, DH), lambda h, *_: (0, h))
    table_spec = pl.BlockSpec((table, DH), lambda h, *_: (0, h))
    return pl.pallas_call(
        attend_kernel,
        grid_spec=pltpu.PrefetchScalarGridSpec(
            num_scalar_prefetch=1,
            grid=(heads,),
            in_specs=[token_spec, table_spec, table_spec, token_spec],
            out_specs=[token_spec, table_spec, table_spec],
            scratch_shapes=[
                pltpu.VMEM((table, DH), jnp.float32),
                pltpu.VMEM((table, DH), jnp.float32),
                pltpu.VMEM((table // BLK, DH, BLK), jnp.bfloat16),
                pltpu.VMEM((key_count * BLK, DH), jnp.bfloat16),
                pltpu.VMEM((key_count * BLK, DH), jnp.bfloat16),
                pltpu.VMEM((DH, key_count * BLK), jnp.bfloat16),
            ],
        ),
        out_shape=[
            jax.ShapeDtypeStruct(query.shape, jnp.bfloat16),
            jax.ShapeDtypeStruct(key.shape, table_type),
            jax.ShapeDtypeStruct(key.shape, table_type),
        ],
        compiler_params=pltpu.CompilerParams(vmem_limit_bytes=VMEM_BYTES),
        name="attend",
    )(index.reshape(-1), query, key, value, grad)


def by_pools(
    queries, key_vecs, value_vecs, out_grads, local_offsets, partner_pool, partner_picks
):
    to_heads = functools.partial(lax.all_to_all, axis_name="head", split_axis=1, concat_axis=0, tiled=True)
    to_tokens = functools.partial(lax.all_to_all, axis_name="head", split_axis=0, concat_axis=1, tiled=True)
    query, key, value, grad = (to_heads(x) for x in (queries, key_vecs, value_vecs, out_grads))
    width = query.shape[1]
    blocks = query.shape[0] // BLK
    bits, pool_size = partner_pool.shape[1:]
    group = lax.axis_index("ctx")
    asked = [partner_pool[jnp.bitwise_xor(group, 1 << bit), bit] for bit in range(bits)]

    def table(array):
        by_block = array.reshape(blocks, BLK, width)
        far = [swapped(by_block[asked[bit]], "ctx", 1 << bit) for bit in range(bits)]
        return jnp.concatenate([by_block] + far).reshape(-1, width)

    inner = jnp.arange(blocks, dtype=jnp.int32)
    own = (inner[:, None] + local_offsets) % blocks
    far = blocks + jnp.arange(bits, dtype=jnp.int32)[None, :, None] * pool_size + partner_picks
    index = jnp.concatenate([own, far.reshape(blocks, -1)], axis=1).astype(jnp.int32)
    dq, *tables = attend(index, query, table(key), table(value), grad, jnp.float32)
    grads = [dq]
    for array in tables:
        by_block = array.reshape(-1, BLK, width)
        total = by_block[:blocks]
        for bit in range(bits):
            lower = blocks + bit * pool_size
            back = swapped(by_block[lower : lower + pool_size], "ctx", 1 << bit)
            total = total.at[asked[bit]].add(back)
        grads.append(total.reshape(blocks * BLK, width).astype(jnp.bfloat16))
    return tuple(to_tokens(x) for x in grads)


def per_device(*args):
    tokens, features = args[0].shape
    parts = lax.axis_size("head")
    cluster = parts << args[5].shape[1]
    if features // DH == cluster and tokens == BLK and parts & (parts - 1) == 0 and 1 < parts <= INDEX_ROWS:
        return whole_cluster(*args)
    return by_pools(*args)


def solution(mesh):
    return jax.shard_map(
        per_device,
        mesh=mesh,
        in_specs=(
            P(("ctx", "head"), None),
            P(("ctx", "head"), None),
            P(("ctx", "head"), None),
            P(("ctx", "head"), None),
            P("ctx", None),
            P(),
            P("ctx", None, None),
        ),
        out_specs=(P(("ctx", "head"), None), P(("ctx", "head"), None), P(("ctx", "head"), None)),
        check_vma=False,
    )
```

```python
import functools

import jax
import jax.numpy as jnp
from jax import lax
from jax.experimental import pallas as pl
from jax.experimental.pallas import tpu as pltpu
from jax.sharding import PartitionSpec as P

DH = 128
BLK = 128
SCALE = DH**-0.5
LOG2_E = 1.4426950408889634
NT = (((1,), (1,)), ((), ()))
TN = (((0,), (0,)), ((), ()))
VMEM_BYTES = 16 << 20
IN_VMEM = pl.BlockSpec(memory_space=pltpu.VMEM)
IN_SMEM = pl.BlockSpec(memory_space=pltpu.SMEM)
IN_HBM = pl.BlockSpec(memory_space=pl.ANY)
INDEX_ROWS = 16


def swapped(value, axis, distance):
    return lax.ppermute(value, axis, [(i, i ^ distance) for i in range(lax.axis_size(axis))])


def rows(block):
    return pl.ds(block * BLK if isinstance(block, int) else pl.multiple_of(block * BLK, BLK), BLK)


def head_lanes(head):
    return pl.ds(pl.multiple_of(head * DH, DH), DH)


def local_call(kernel, out_shape, scalars, arrays, scratch=(), flops=0, arrays_in=IN_VMEM, vmem_bytes=VMEM_BYTES):
    moved = sum(x.size * x.dtype.itemsize for x in (*arrays, *jax.tree.leaves(out_shape)))
    return pl.pallas_call(
        kernel,
        out_shape=out_shape,
        in_specs=[IN_SMEM] * len(scalars) + [arrays_in] * len(arrays),
        out_specs=jax.tree.map(lambda _: IN_VMEM, out_shape),
        scratch_shapes=list(scratch),
        compiler_params=pltpu.CompilerParams(vmem_limit_bytes=vmem_bytes),
        cost_estimate=pl.CostEstimate(flops=flops, bytes_accessed=moved, transcendentals=0),
        name=getattr(kernel, "func", kernel).__name__,
    )(*scalars, *arrays)


def parts_of(blocks, count, extra=0):
    return [jax.ShapeDtypeStruct((blocks * BLK + extra, DH), jnp.bfloat16)] * count


def natural(me_ref, i, n, by, near):
    k, j = (i, n) if by == "ctx" else (n, i)
    return jnp.bitwise_xor(me_ref[1], j) * near + jnp.bitwise_xor(me_ref[0], k)


def pack(me_ref, *refs, arrays, others, by, near):
    ins, outs = refs[:arrays], refs[arrays:]
    for i, out in enumerate(outs):
        for n in range(others):
            lanes = head_lanes(natural(me_ref, i, n, by, near))
            for place, ref in enumerate(ins):
                out[rows(place * others + n), :] = ref[:, lanes]


def pack_with_index(me_ref, offsets_ref, pool_ref, picks_ref, *refs, parts, near, **kwargs):
    pack(me_ref, *refs, by="ctx", near=near, **kwargs)
    row = lax.broadcasted_iota(jnp.int32, (INDEX_ROWS, DH), 0)
    lane = lax.broadcasted_iota(jnp.int32, (INDEX_ROWS, DH), 1)
    tile = jnp.zeros((INDEX_ROWS, DH), jnp.int32)
    for block in range(parts):
        local = [offsets_ref[block, n] for n in range(offsets_ref.shape[1])]
        chosen = [jnp.bitwise_and(block + offset, parts - 1) * near + me_ref[0] for offset in local]
        for bit in range(picks_ref.shape[1]):
            far = jnp.bitwise_xor(me_ref[0], 1 << bit)
            for n in range(picks_ref.shape[2]):
                chosen.append(pool_ref[me_ref[2], bit, picks_ref[block, bit, n]] * near + far)
        for n, value in enumerate(chosen):
            tile = jnp.where((row == block) & (lane == n), value, tile)
    for out in refs[kwargs["arrays"] :]:
        out[out.shape[0] - INDEX_ROWS :, :] = tile.astype(jnp.float32).astype(out.dtype)


def unpack(me_ref, *refs, by, near):
    *ins, out = refs
    for i, ref in enumerate(ins):
        for n in range(ref.shape[0] // BLK):
            out[:, head_lanes(natural(me_ref, i, n, by, near))] = ref[rows(n), :]


def pack_natural(*refs):
    *ins, out, copied = refs
    copies = []
    for head in range(ins[0].shape[1] // DH):
        for place, ref in enumerate(ins):
            target = head * len(ins) + place
            source = ref.at[:, head * DH : (head + 1) * DH]
            copies.append(pltpu.make_async_copy(source, out.at[rows(target), :], copied.at[target]))
    for copy in copies:
        copy.start()
    for copy in copies:
        copy.wait()


def unpack_natural(ref, *outs):
    for head in range(outs[0].shape[1] // DH):
        for place, out in enumerate(outs):
            out[:, head * DH : (head + 1) * DH] = ref[rows(head * len(outs) + place), :]


def regroup(*refs, count, places):
    ins, outs = refs[:count], refs[count:]
    for i, out in enumerate(outs):
        for n, place in enumerate(places):
            for k, ref in enumerate(ins):
                out[rows(n * count + k), :] = ref[rows(place * len(outs) + i), :]


def regroup_with_index(*refs, count, places):
    *refs, index_ref = refs
    regroup(*refs, count=count, places=places)
    for k, ref in enumerate(refs[:count]):
        tile = ref[ref.shape[0] - INDEX_ROWS :, :]
        index_ref[k * INDEX_ROWS : (k + 1) * INDEX_ROWS, :] = tile.astype(jnp.float32).astype(jnp.int32)


def gather(me_ref, table, refs, by, near, place=0):
    others = table.shape[0] // len(refs)
    for i, ref in enumerate(refs):
        for n in range(others):
            table[natural(me_ref, i, n, by, near)] = ref[rows(place * others + n), :]


def spread(me_ref, table, refs, by, near):
    others = table.shape[0] // len(refs)
    for i, ref in enumerate(refs):
        for n in range(others):
            ref[rows(n), :] = table[natural(me_ref, i, n, by, near)].astype(ref.dtype)


def chosen_blocks(me_ref, index_ref, block, near, key_count):
    group = jnp.bitwise_xor(lax.rem(block, near), me_ref[0])
    row = group * INDEX_ROWS + lax.div(block, near)
    return [index_ref[row, j] for j in range(key_count)]


def pair_of(block_of, first, second):
    return jnp.concatenate(
        [jnp.concatenate([block_of(a), block_of(b)], axis=1) for a, b in zip(first, second, strict=True)], axis=0
    )


def set_diagonal(ref, first, second):
    ref[:BLK, :DH] = first
    ref[BLK:, DH:] = second


def add_pair(acc, chosen, values):
    for half, blocks in enumerate(chosen):
        for j, block in enumerate(blocks):
            acc[block] += values[j * BLK : (j + 1) * BLK, half * DH : (half + 1) * DH]


def for_pairs(me_ref, index_ref, count, near, key_count, unroll, one):
    def step(i, _):
        for slot in range(unroll):
            pair = i * unroll + slot
            blocks = (2 * pair, 2 * pair + 1)
            one(pair, slot, blocks, [chosen_blocks(me_ref, index_ref, b, near, key_count) for b in blocks])
        return 0

    lax.fori_loop(0, count // unroll, step, 0)


def joined_block(ref, blocks, place):
    arrays = ref.shape[0] // (blocks * BLK)
    return lambda b: ref[rows(b * arrays + place), :]


def softmax_weights(me_ref, index_ref, joined_ref, w_ref, half_ref, q_diag, *, parts, near, key_count, unroll):
    query, key = (joined_block(joined_ref, near * parts, place) for place in range(2))
    q_diag[...] = jnp.zeros_like(q_diag)

    def one(pair, slot, blocks, chosen):
        set_diagonal(q_diag.at[slot], *map(query, blocks))
        keys = pair_of(key, *chosen)
        scores = lax.dot_general(keys, q_diag[slot], NT, preferred_element_type=jnp.float32)
        row_max = jnp.max(scores, axis=0, keepdims=True)
        exp_scores = jnp.exp2((scores - row_max) * (SCALE * LOG2_E))
        weights = exp_scores * (1.0 / jnp.sum(exp_scores, axis=0, keepdims=True))
        w_ref[pair] = weights * SCALE
        half_ref[pair] = weights.astype(half_ref.dtype)

    for_pairs(me_ref, index_ref, w_ref.shape[0], near, key_count, unroll, one)


def dv_parts(me_ref, index_ref, half_ref, *refs, parts, near, key_count, unroll):
    g_refs, dv_refs, (acc, g_table, g_diag) = refs[:parts], refs[parts : 2 * parts], refs[2 * parts :]
    gather(me_ref, g_table, g_refs, "head", near)
    for ref in (acc, g_diag):
        ref[...] = jnp.zeros_like(ref)

    def one(pair, slot, blocks, chosen):
        set_diagonal(g_diag.at[slot], *(g_table[b] for b in blocks))
        add_pair(acc, chosen, jnp.dot(half_ref[pair], g_diag[slot], preferred_element_type=jnp.float32))

    for_pairs(me_ref, index_ref, half_ref.shape[0], near, key_count, unroll, one)
    spread(me_ref, acc, dv_refs, "head", near)


def dq_and_dk(me_ref, index_ref, joined_ref, *refs, parts, near, key_count, unroll):
    g_refs, v_refs, refs = refs[:parts], refs[parts : 2 * parts], refs[2 * parts :]
    w_ref, out_ref, acc, g_table, v_table, q_diag, g_diag = refs
    gather(me_ref, g_table, g_refs, "head", near)
    gather(me_ref, v_table, v_refs, "head", near)
    for ref in (acc, q_diag, g_diag):
        ref[...] = jnp.zeros_like(ref)
    query, key = (joined_block(joined_ref, near * parts, place) for place in range(2))

    def one(pair, slot, blocks, chosen):
        set_diagonal(q_diag.at[slot], *map(query, blocks))
        set_diagonal(g_diag.at[slot], *(g_table[b] for b in blocks))
        values = pair_of(lambda b: v_table[b], *chosen)
        prob_grad = lax.dot_general(values, g_diag[slot], NT, preferred_element_type=jnp.float32)
        scaled = w_ref[pair]
        row_delta = jnp.sum(scaled * prob_grad, axis=0, keepdims=True) * (1 / SCALE)
        score_grad = (scaled * (prob_grad - row_delta)).astype(jnp.bfloat16)
        add_pair(acc, chosen, jnp.dot(score_grad, q_diag[slot], preferred_element_type=jnp.float32))
        keys = pair_of(key, *chosen)
        grads = lax.dot_general(score_grad, keys, TN, preferred_element_type=jnp.float32)
        for half, block in enumerate(blocks):
            own = slice(half * BLK, (half + 1) * BLK)
            out_ref[rows(2 * block), :] = grads[own, own].astype(out_ref.dtype)

    for_pairs(me_ref, index_ref, w_ref.shape[0], near, key_count, unroll, one)
    for block in range(acc.shape[0]):
        out_ref[rows(2 * block + 1), :] = acc[block].astype(out_ref.dtype)


def whole_cluster(
    queries, key_vecs, value_vecs, out_grads, local_offsets, partner_pool, partner_picks
):
    bits = partner_pool.shape[1]
    parts = lax.axis_size("head")
    near = 1 << bits
    cluster = near * parts
    key_count = local_offsets.shape[1] + bits * partner_picks.shape[2]
    group = lax.axis_index("ctx")
    me = jnp.stack([jnp.bitwise_and(group, near - 1), lax.axis_index("head"), group]).astype(jnp.int32)

    def over_ctx(by_part):
        return [x if k == 0 else swapped(x, "ctx", k) for k, x in enumerate(by_part)]

    def over_head(by_part):
        return [x if j == 0 else swapped(x, "head", j) for j, x in enumerate(by_part)]

    members = [
        [member * parts + part for part in range(parts) for member in range(first, first + near)]
        for first in range(0, lax.axis_size("ctx"), near)
    ]
    exchange = functools.partial(
        lax.all_to_all, axis_name=("ctx", "head"), split_axis=0, concat_axis=0, tiled=True, axis_index_groups=members
    )
    joined = local_call(
        pack_natural,
        parts_of(2 * cluster, 1)[0],
        (),
        (queries, key_vecs),
        [pltpu.SemaphoreType.DMA((2 * cluster,))],
        arrays_in=IN_HBM,
        vmem_bytes=58 << 20,
    )
    later = (out_grads, value_vecs, local_offsets, partner_pool, partner_picks)
    joined, later = lax.optimization_barrier((joined, later))
    out_grads, value_vecs, local_offsets, partner_pool, partner_picks = later
    joined = exchange(joined)
    grad = local_call(
        functools.partial(pack, arrays=1, others=parts, by="ctx", near=near), parts_of(parts, near), (me,), (out_grads,)
    )
    grad = local_call(functools.partial(regroup, count=near, places=[0]), parts_of(near, parts), (), over_ctx(grad))
    grad = over_head(grad)
    value = local_call(
        functools.partial(pack_with_index, arrays=1, others=parts, parts=parts, near=near),
        parts_of(parts, near, INDEX_ROWS),
        (me, local_offsets, partner_pool, partner_picks),
        (value_vecs,),
    )
    *value, index = local_call(
        functools.partial(regroup_with_index, count=near, places=[0]),
        parts_of(near, parts) + [jax.ShapeDtypeStruct((near * INDEX_ROWS, DH), jnp.int32)],
        (),
        over_ctx(value),
    )
    middle, last = parts // 2, parts - 1
    value[middle], grad[last] = lax.optimization_barrier((value[middle], grad[last]))
    value = over_head(value)

    pairs, keys = cluster // 2, key_count * BLK
    unroll = next(n for n in (8, 4, 2, 1) if pairs % n == 0)
    kwargs = dict(parts=parts, near=near, key_count=key_count, unroll=unroll)
    flops = 4 * cluster * keys * BLK * DH
    acc, table = (pltpu.VMEM((cluster, BLK, DH), dtype) for dtype in (jnp.float32, jnp.bfloat16))
    diagonal = pltpu.VMEM((unroll, 2 * BLK, 2 * DH), jnp.bfloat16)
    weights, half = local_call(
        functools.partial(softmax_weights, **kwargs),
        [jax.ShapeDtypeStruct((pairs, keys, 2 * BLK), dtype) for dtype in (jnp.float32, jnp.bfloat16)],
        (me, index),
        (joined,),
        [diagonal],
        flops // 2,
    )
    dv = local_call(
        functools.partial(dv_parts, **kwargs),
        parts_of(near, parts),
        (me, index),
        (half, *grad),
        [acc, table, diagonal],
        flops // 2,
    )
    dv = over_head(dv)
    joined = local_call(
        functools.partial(dq_and_dk, **kwargs),
        parts_of(2 * cluster, 1)[0],
        (me, index),
        (joined, *grad, *value, weights),
        [acc] + [table] * 2 + [diagonal] * 2,
        flops * 3 // 2,
    )
    joined, dv = lax.optimization_barrier((joined, dv))
    joined = exchange(joined)
    dv = local_call(functools.partial(regroup, count=parts, places=[0]), parts_of(parts, near), (), dv)
    dv = over_ctx(dv)
    out = jax.ShapeDtypeStruct(queries.shape, queries.dtype)
    value_grads = local_call(functools.partial(unpack, by="ctx", near=near), out, (me,), dv)
    query_grads, key_grads = local_call(unpack_natural, [out] * 2, (), (joined,))
    return query_grads, key_grads, value_grads


def attend_kernel(
    index_ref, q_ref, k_ref, v_ref, g_ref, dq_ref, dk_ref, dv_ref, acc_k, acc_v, k_turned, k_cat, v_cat, kt_cat
):
    query_blocks = q_ref.shape[0] // BLK
    table_blocks = k_ref.shape[0] // BLK
    key_count = k_cat.shape[0] // BLK

    acc_k[...] = jnp.zeros_like(acc_k)
    acc_v[...] = jnp.zeros_like(acc_v)
    for block in range(table_blocks):
        k_turned[block] = k_ref[block * BLK : (block + 1) * BLK, :].T

    def step(block, _):
        query = q_ref[rows(block), :]
        grad = g_ref[rows(block), :]
        chosen = [index_ref[block * key_count + j] for j in range(key_count)]
        for j in range(key_count):
            part = slice(j * BLK, (j + 1) * BLK)
            k_cat[part, :] = k_ref[rows(chosen[j]), :]
            v_cat[part, :] = v_ref[rows(chosen[j]), :]
            kt_cat[:, part] = k_turned[chosen[j]]
        scores = lax.dot_general(k_cat[...], query, NT, preferred_element_type=jnp.float32)
        row_max = jnp.max(scores, axis=0, keepdims=True)
        exp_scores = jnp.exp2((scores - row_max) * (SCALE * LOG2_E))
        weights = exp_scores * (1.0 / jnp.sum(exp_scores, axis=0, keepdims=True))
        prob_grad = lax.dot_general(v_cat[...], grad, NT, preferred_element_type=jnp.float32)
        row_delta = jnp.sum(weights * prob_grad, axis=0, keepdims=True)
        score_grad = (SCALE * weights * (prob_grad - row_delta)).astype(jnp.bfloat16)
        weights_half = weights.astype(jnp.bfloat16)
        query_turned = jnp.dot(kt_cat[...], score_grad, preferred_element_type=jnp.float32)
        dq_ref[rows(block), :] = query_turned.T.astype(jnp.bfloat16)
        key_out = jnp.dot(score_grad, query, preferred_element_type=jnp.float32)
        value_out = jnp.dot(weights_half, grad, preferred_element_type=jnp.float32)
        for j in range(key_count):
            part = slice(j * BLK, (j + 1) * BLK)
            acc_k[rows(chosen[j]), :] += key_out[part]
            acc_v[rows(chosen[j]), :] += value_out[part]
        return 0

    lax.fori_loop(0, query_blocks, step, 0)
    dk_ref[...] = acc_k[...].astype(dk_ref.dtype)
    dv_ref[...] = acc_v[...].astype(dv_ref.dtype)


def attend(index, query, key, value, grad, table_type):
    heads = query.shape[1] // DH
    key_count = index.shape[1]
    tokens, table = query.shape[0], key.shape[0]
    token_spec = pl.BlockSpec((tokens, DH), lambda h, *_: (0, h))
    table_spec = pl.BlockSpec((table, DH), lambda h, *_: (0, h))
    return pl.pallas_call(
        attend_kernel,
        grid_spec=pltpu.PrefetchScalarGridSpec(
            num_scalar_prefetch=1,
            grid=(heads,),
            in_specs=[token_spec, table_spec, table_spec, token_spec],
            out_specs=[token_spec, table_spec, table_spec],
            scratch_shapes=[
                pltpu.VMEM((table, DH), jnp.float32),
                pltpu.VMEM((table, DH), jnp.float32),
                pltpu.VMEM((table // BLK, DH, BLK), jnp.bfloat16),
                pltpu.VMEM((key_count * BLK, DH), jnp.bfloat16),
                pltpu.VMEM((key_count * BLK, DH), jnp.bfloat16),
                pltpu.VMEM((DH, key_count * BLK), jnp.bfloat16),
            ],
        ),
        out_shape=[
            jax.ShapeDtypeStruct(query.shape, jnp.bfloat16),
            jax.ShapeDtypeStruct(key.shape, table_type),
            jax.ShapeDtypeStruct(key.shape, table_type),
        ],
        compiler_params=pltpu.CompilerParams(vmem_limit_bytes=VMEM_BYTES),
        name="attend",
    )(index.reshape(-1), query, key, value, grad)


def by_pools(
    queries, key_vecs, value_vecs, out_grads, local_offsets, partner_pool, partner_picks
):
    to_heads = functools.partial(lax.all_to_all, axis_name="head", split_axis=1, concat_axis=0, tiled=True)
    to_tokens = functools.partial(lax.all_to_all, axis_name="head", split_axis=0, concat_axis=1, tiled=True)
    query, key, value, grad = (to_heads(x) for x in (queries, key_vecs, value_vecs, out_grads))
    width = query.shape[1]
    blocks = query.shape[0] // BLK
    bits, pool_size = partner_pool.shape[1:]
    group = lax.axis_index("ctx")
    asked = [partner_pool[jnp.bitwise_xor(group, 1 << bit), bit] for bit in range(bits)]

    def table(array):
        by_block = array.reshape(blocks, BLK, width)
        far = [swapped(by_block[asked[bit]], "ctx", 1 << bit) for bit in range(bits)]
        return jnp.concatenate([by_block] + far).reshape(-1, width)

    inner = jnp.arange(blocks, dtype=jnp.int32)
    own = (inner[:, None] + local_offsets) % blocks
    far = blocks + jnp.arange(bits, dtype=jnp.int32)[None, :, None] * pool_size + partner_picks
    index = jnp.concatenate([own, far.reshape(blocks, -1)], axis=1).astype(jnp.int32)
    dq, *tables = attend(index, query, table(key), table(value), grad, jnp.float32)
    grads = [dq]
    for array in tables:
        by_block = array.reshape(-1, BLK, width)
        total = by_block[:blocks]
        for bit in range(bits):
            lower = blocks + bit * pool_size
            back = swapped(by_block[lower : lower + pool_size], "ctx", 1 << bit)
            total = total.at[asked[bit]].add(back)
        grads.append(total.reshape(blocks * BLK, width).astype(jnp.bfloat16))
    return tuple(to_tokens(x) for x in grads)


def per_device(*args):
    tokens, features = args[0].shape
    parts = lax.axis_size("head")
    cluster = parts << args[5].shape[1]
    if features // DH == cluster and tokens == BLK and parts & (parts - 1) == 0 and 1 < parts <= INDEX_ROWS:
        return whole_cluster(*args)
    return by_pools(*args)


def solution(mesh):
    return jax.shard_map(
        per_device,
        mesh=mesh,
        in_specs=(
            P(("ctx", "head"), None),
            P(("ctx", "head"), None),
            P(("ctx", "head"), None),
            P(("ctx", "head"), None),
            P("ctx", None),
            P(),
            P("ctx", None, None),
        ),
        out_specs=(P(("ctx", "head"), None), P(("ctx", "head"), None), P(("ctx", "head"), None)),
        check_vma=False,
    )
```
